256 devices in a mesh: seg: 64 (over x, z, core), sub: 4 (over y).
Axes of the slice: x: 4, y: 4, z: 8, core: 2. Of those that a mesh axis runs over, the one named last changes fastest.
Arguments:
- rhs_local: float32 [64, 4, 16, 32, 128], P('seg', 'sub'), may hold values from -6 to 6
- diag_inv: float32 [64, 4, 16, 128, 128], P('seg', 'sub')
- off_blocks: float32 [64, 4, 16, 4, 128, 128], P('seg', 'sub'), may hold values from -0.08 to 0.08
- pattern: int32 [64, 4, 16, 4], P('seg', 'sub'), may hold values from -1 to 17, as said below
- sep_rhs: float32 [64, 32, 128], P('seg'), may hold values from -6 to 6
- sep_inv: float32 [64, 128, 128], P('seg')
- coupling: float32 [64, 128, 128], P('seg'), may hold values from -0.4375 to 0.4375
Outputs:
- tree_solution: float32 [64, 4, 16, 32, 128], P('seg', 'sub')
- sep_solution: float32 [64, 32, 128], P('seg')
The draws below stay inside these ranges and needn't reach their ends.
Inputs may be any that keep to these rules, and one draw needn't show every extreme that they name: In each row pattern[s, u, j], every entry is -1 (empty slot) or a target greater than j, and the filled targets of one row are distinct.
All inputs are finite; a program needn't handle non-finite values.
Results may differ from the reference program's by a relative error of at most 0.0003.
Values sent between devices are 32-bit elements; how exact they have to be, the bound alone decides.
A program may use at most 64 MiB of HBM per device.

```python
import math
import jax
import jax.numpy as jnp
from jax import lax

W = 128
R = 32
KB = 4
LOC = 16
SEGS = 64
SUBS = 4


def triangle(key, grid_shape):
    first_key, second_key = jax.random.split(key)
    row_ids = lax.broadcasted_iota(jnp.int32, grid_shape, len(grid_shape) - 2)
    col_ids = lax.broadcasted_iota(jnp.int32, grid_shape, len(grid_shape) - 1)
    below_part = jax.random.normal(first_key, grid_shape, jnp.float32) * (0.5 / math.sqrt(W))
    middle = jax.random.uniform(second_key, grid_shape, jnp.float32, 0.6, 1.4)
    return jnp.where(row_ids > col_ids, below_part, jnp.where(row_ids == col_ids, middle, 0.0))


def draw_diag_inv(key, part):
    return triangle(key, (SEGS, SUBS, LOC, W, W))


def draw_sep_inv(key, part):
    return triangle(key, (SEGS, W, W))


def draw_off_blocks(key, part):
    key = jax.random.fold_in(key, 5)
    grid_shape = (SEGS, SUBS, LOC, KB, W, W)
    values = jnp.clip(jax.random.normal(key, grid_shape, jnp.float32) * 0.036, -0.08, 0.08)
    return values


def draw_pattern(key, part):
    grid_shape = (SEGS, SUBS, LOC, LOC + 2)
    target_ids = lax.broadcasted_iota(jnp.int32, grid_shape, 3)
    source_ids = lax.broadcasted_iota(jnp.int32, grid_shape, 2)
    scores = jax.random.randint(key, grid_shape, 0, 1 << 20, jnp.int32) * (LOC + 2) + target_ids
    allowed = target_ids > source_ids
    ranked = jnp.where(allowed, scores, (1 << 30) + target_ids)
    values, chosen = lax.top_k(-ranked, KB)
    return jnp.where(-values < 1 << 30, chosen, -1).astype(jnp.int32)


def block_scale(rng, dims, shards, low, top_value):
    def one(dim, parts):
        steps = jax.random.uniform(jax.random.fold_in(jax.random.fold_in(rng, 6), dim), (parts,), jnp.float32, low / len(shards), top_value / len(shards))
        return jnp.repeat(jnp.exp(steps), dims[dim] // parts).reshape((-1,) + (1,) * (len(dims) - dim - 1))

    factor_of = one(*shards[0])
    for cut in shards[1:]:
        factor_of = factor_of * one(*cut)
    return factor_of


def gaussian(rng, extent, deviation, limit, shards=(), held_as=jnp.bfloat16):
    drawn = jax.random.normal(rng, extent, jnp.float32) * deviation
    if len(shards) > 0:
        drawn = block_scale(rng, extent, shards, -0.22, 0.18) * drawn
    return jnp.clip(drawn, min=-limit, max=limit).astype(held_as)


def setup_inputs(seed: int = 0) -> dict:
    seeds = jax.random.split(jax.random.key(seed), 8)
    return {
        "rhs_local": gaussian(seeds[0], (SEGS, SUBS, LOC, R, W), 1.0, 6.0, ((0, 64), (1, 4)), jnp.float32),
        "diag_inv": draw_diag_inv(jax.random.fold_in(seeds[7], 71), 0),
        "off_blocks": draw_off_blocks(jax.random.fold_in(seeds[7], 71), 0),
        "pattern": draw_pattern(jax.random.fold_in(seeds[7], 71), 0),
        "sep_rhs": gaussian(seeds[4], (SEGS, R, W), 1.0, 6.0, ((0, 64),), jnp.float32),
        "sep_inv": draw_sep_inv(jax.random.fold_in(seeds[7], 71), 0),
        "coupling": gaussian(seeds[6], (SEGS, W, W), ((4 * W) // 3) ** -0.5, 0.4375, ((0, 64),), jnp.float32),
    }


HIGH = lax.Precision.HIGHEST


def tree_down(source, inverse, blocks, targets):
    supernodes = source.shape[0]
    updates = jnp.zeros((supernodes + 2,) + source.shape[1:], jnp.float32)
    solved = jnp.zeros_like(source)

    def advance(position, state_pair):
        solved, updates = state_pair
        remain = source[position] - updates[position]
        column = jnp.einsum('rb,ab->ra', remain, inverse[position], precision=HIGH)
        products = jnp.einsum('rc,kac->kra', column, blocks[position], precision=HIGH)
        row_targets = targets[position]
        for slot_number in range(row_targets.shape[0]):
            target = jnp.maximum(row_targets[slot_number], 0).astype(jnp.int32)
            weight_on = (row_targets[slot_number] >= 0).astype(products.dtype)
            current = lax.dynamic_index_in_dim(updates, target, 0, keepdims=False)
            updates = lax.dynamic_update_index_in_dim(updates, current + weight_on * products[slot_number], target, 0)
        solved = lax.dynamic_update_index_in_dim(solved, column, position, 0)
        return solved, updates

    solved, updates = lax.fori_loop(0, supernodes, advance, (solved, updates))
    return solved, updates[supernodes], updates[supernodes + 1]


def tree_up(solved, inverse, blocks, targets, own_sep, left_sep):
    supernodes = solved.shape[0]
    known_rows = jnp.concatenate([jnp.zeros_like(solved), own_sep[None], left_sep[None]], 0)

    def retreat(offset, known_rows):
        position = supernodes - 1 - offset
        row_targets = targets[position]
        weight_on = (row_targets >= 0).astype(known_rows.dtype)[:, None, None]
        picked = known_rows[jnp.maximum(row_targets, 0).astype(jnp.int32)] * weight_on
        pulled = jnp.einsum('kra,kac->rc', picked, blocks[position], precision=HIGH)
        column = jnp.einsum('ra,ac->rc', solved[position] - pulled, inverse[position], precision=HIGH)
        return lax.dynamic_update_index_in_dim(known_rows, column, position, 0)

    known_rows = lax.fori_loop(0, supernodes, retreat, known_rows)
    return known_rows[:supernodes]


def reference(rhs_local, diag_inv, off_blocks, pattern, sep_rhs, sep_inv, coupling):
    def flatten(array):
        return array.reshape((SEGS * SUBS,) + array.shape[2:])

    def down_one(inputs):
        return tree_down(*inputs)

    tree_forward, own_terms, left_terms = lax.map(down_one, (flatten(rhs_local), flatten(diag_inv), flatten(off_blocks), flatten(pattern)))
    own_total = own_terms.reshape((SEGS, SUBS) + own_terms.shape[1:]).sum(1)
    left_total = left_terms.reshape((SEGS, SUBS) + left_terms.shape[1:]).sum(1)
    zero_rows = jnp.zeros((1,) + sep_rhs.shape[1:], jnp.float32)
    left_next = jnp.concatenate([left_total[1:], zero_rows], 0)
    reduced = sep_rhs - own_total - left_next

    def forward(previous, inputs):
        rhs_part, inverse, link = inputs
        remain = rhs_part - jnp.einsum('rc,ac->ra', previous, link, precision=HIGH)
        current = jnp.einsum('rb,ab->ra', remain, inverse, precision=HIGH)
        return current, current

    _, sep_forward = lax.scan(forward, zero_rows[0], (reduced, sep_inv, coupling))
    link_next = jnp.concatenate([coupling[1:], jnp.zeros((1,) + coupling.shape[1:], jnp.float32)], 0)

    def backward(following, inputs):
        rhs_part, inverse, link = inputs
        remain = rhs_part - jnp.einsum('ra,ac->rc', following, link, precision=HIGH)
        current = jnp.einsum('ra,ac->rc', remain, inverse, precision=HIGH)
        return current, current

    _, sep_solution = lax.scan(backward, zero_rows[0], (sep_forward, sep_inv, link_next), reverse=True)
    left_solution = jnp.concatenate([zero_rows, sep_solution[:-1]], 0)
    own_each = jnp.repeat(sep_solution, SUBS, axis=0)
    left_each = jnp.repeat(left_solution, SUBS, axis=0)

    def up_one(inputs):
        return tree_up(*inputs)

    tree_solution = lax.map(up_one, (tree_forward, flatten(diag_inv), flatten(off_blocks), flatten(pattern), own_each, left_each))
    return tree_solution.reshape(rhs_local.shape), sep_solution
```

```python
import jax
import jax.numpy as jnp
from jax import lax
from jax.experimental import pallas as pl
from jax.experimental.pallas import tpu as pltpu
from jax.sharding import PartitionSpec as P

BF = jnp.bfloat16
F32 = jnp.float32
MESH = pl.DeviceIdType.MESH
LOC, KB, R, W = 16, 4, 32, 128
SEGS, SUBS = 64, 4
RING, CHIPS, ROWS = 16, 8, 8


def halves(v):
    high = v.astype(BF)
    return high, (v - high.astype(F32)).astype(BF)


def left_operand(v):
    high, low = halves(v)
    top = jnp.concatenate([high, high], 1)
    bottom = jnp.concatenate([low, jnp.zeros_like(low)], 1)
    return jnp.concatenate([top, bottom], 0)


def folded(left, right, dims):
    both = lax.dot_general(left, right, (dims, ((), ())), preferred_element_type=F32)
    half = both.shape[0] // 2
    return both[:half] + both[half:]


def times(v, w):
    high, low = halves(w)
    return folded(left_operand(v), jnp.concatenate([high, low], 0), ((1,), (0,)))


def times_t(v, w):
    high, low = halves(w)
    return folded(left_operand(v), jnp.concatenate([high, low], 1), ((1,), (1,)))


def t_times(w, v):
    return times(w.T, v)


def chain_kernel(
    pat, rhs_hbm, inv_hbm, off_hbm, sep_rhs_hbm, sep_inv_hbm, coupling_hbm,
    y_ref, own_ref, left_ref,
    rhs, sep_rhs, sep_inv, coupling, small_sem,
    inv, off, acc, vpair, vq, part, xg, rown, rleft, xs, xl, suf_v, suf_q, suf_w, pre_v, pre_z, ends,
    inv_sem, off_sem, pair_ss, pair_rs, z_ss, z_rs, f_ss, f_rs, ring_ss, ring_rs, x_ss, x_rs,
    red_ss, red_rs, lft_ss, lft_rs, fin_ss, fin_rs, nxt_ss, nxt_rs,
):
    s = lax.axis_index("seg")
    u = lax.axis_index("sub")
    core = s % 2
    m = (s // 2) % CHIPS
    i = s % RING
    g = s // RING
    base = s - i

    def send(src, dst, ss, rs, target):
        copy = pltpu.make_async_remote_copy(
            src_ref=src, dst_ref=dst, send_sem=ss, recv_sem=rs, device_id=target, device_id_type=MESH
        )
        copy.start()
        return copy

    def local(hbm, vmem, sem):
        copy = pltpu.make_async_copy(hbm, vmem, sem)
        copy.start()
        return copy

    sibling = (s + 1 - 2 * core, u)
    after = lax.rem(s + 1, SEGS)
    before = lax.rem(s + SEGS - 1, SEGS)

    def ring_peer(k):
        return (base + lax.rem(i + k, RING), u)

    def chip_peer(k):
        return (base + lax.rem(i + 2 * k, RING), u)

    def plane_peer(k):
        return (lax.rem(s + RING * k, SEGS), u)

    def sub_peer(k):
        return (s, lax.rem(u + k, SUBS))

    barrier = pltpu.get_barrier_semaphore()
    greeted = [ring_peer(k) for k in range(1, RING)]
    greeted += [plane_peer(k) for k in range(1, 4)]
    greeted += [sub_peer(k) for k in range(1, SUBS)]
    greeted += [(after, v) for v in range(SUBS)] + [(before, v) for v in range(SUBS)]
    for peer in greeted:
        pl.semaphore_signal(barrier, inc=1, device_id=peer, device_id_type=MESH)

    sep_inv_copy = local(sep_inv_hbm, sep_inv, small_sem.at[0])
    coupling_copy = local(coupling_hbm, coupling, small_sem.at[1])
    rhs_copy = local(rhs_hbm, rhs, small_sem.at[2])
    sep_rhs_copy = local(sep_rhs_hbm, sep_rhs, small_sem.at[3])
    inv_copies = []
    off_copies = []
    for j in range(LOC):
        inv_copies.append(local(inv_hbm.at[j], inv.at[j], inv_sem.at[j]))
        off_copies.append(local(off_hbm.at[j], off.at[j], off_sem.at[j]))

    sep_inv_copy.wait()
    coupling_copy.wait()
    dinv = sep_inv[...]
    own_v = -times(dinv, coupling[...]).T
    own_v = jnp.where(s > 0, own_v, 0.0)
    vpair[core] = own_v

    acc[...] = jnp.zeros_like(acc)
    rhs_copy.wait()

    def down(j):
        inv_copies[j].wait()
        off_copies[j].wait()
        y = times_t(rhs[j] - acc[j].reshape(R, W), inv[j])
        y_ref[j] = y
        products = times_t(y, off[j].reshape(KB * W, W))
        width = LOC + 1 - j
        ids = lax.broadcasted_iota(jnp.int32, (width, 1, ROWS, W), 0) + (j + 1)
        total = acc[j + 1 :]
        for k in range(KB):
            piece = products[:, k * W : (k + 1) * W].reshape(1, SUBS, ROWS, W)
            total = total + jnp.where(ids == pat[k, j], piece, 0.0)
        acc[j + 1 :] = total

    for j in range(0, 8):
        down(j)

    pl.semaphore_wait(barrier, len(greeted))
    pair_copy = send(vpair.at[core], vpair.at[core], pair_ss, pair_rs, sibling)
    for j in range(8, 11):
        down(j)
    pair_copy.wait_recv()
    v0 = vpair[0]
    v1 = vpair[1]
    vm = times(v0, v1)
    vq[m, 0] = vm
    vq[m, 1] = times_t(v0, v0) + times_t(vm, vm)
    z_copies = []
    for k in (4, 3, 5, 2, 6, 1, 7):
        z_copies.append(send(vq.at[m, core], vq.at[m, core], z_ss.at[k - 1], z_rs.at[k - 1], chip_peer(k)))
    for j in range(11, LOC):
        down(j)

    red_copies = []
    for k in range(1, SUBS):
        peer = sub_peer(k)
        red_copies.append(send(acc.at[LOC, peer[1]], rown.at[u], red_ss.at[k - 1], red_rs.at[k - 1], peer))
    for k in range(SUBS):
        v = lax.rem(u + k, SUBS)
        red_copies.append(send(acc.at[LOC + 1, v], rleft.at[u], lft_ss.at[k], lft_rs.at[k], (before, v)))
    rown[u] = acc[LOC, u]
    for copy in red_copies:
        copy.wait_recv()
    sep_rhs_copy.wait()
    left_sum = (rleft[0] + rleft[1]) + (rleft[2] + rleft[3])
    reduced = sep_rhs[u] - ((rown[0] + rown[1]) + (rown[2] + rown[3])) - jnp.where(s < SEGS - 1, left_sum, 0.0)
    phi = times_t(reduced, dinv)
    phi_part = jnp.where(core == 0, times(phi, v1), phi)
    part[i, 0] = phi_part
    part[i, 1] = jnp.where(core == 0, times_t(phi, v0), 0.0) + times_t(phi_part, vm)
    part[i, 2] = phi
    ring_copies = []
    for k in range(1, RING):
        ring_copies.append(send(part.at[i], part.at[i], ring_ss.at[k - 1], ring_rs.at[k - 1], ring_peer(k)))

    f_copies = []
    for copy, k in reversed(list(zip(z_copies, (4, 3, 5, 2, 6, 1, 7)))):
        copy.wait_recv()
        source = lax.rem(m + CHIPS - k, CHIPS)
        f_copies.append(
            send(vq.at[source, core], vq.at[source, core], f_ss.at[k - 1], f_rs.at[k - 1], sibling)
        )
    for copy in ring_copies:
        copy.wait_recv()
    for copy in f_copies:
        copy.wait_recv()

    eye = (
        lax.broadcasted_iota(jnp.int32, (W, W), 0) == lax.broadcasted_iota(jnp.int32, (W, W), 1)
    ).astype(F32)
    suf_v[CHIPS] = eye
    suf_q[CHIPS] = jnp.zeros((W, W), F32)
    suf_w[CHIPS] = jnp.zeros((ROWS, W), F32)
    pre_v[0] = eye
    pre_z[0] = jnp.zeros((ROWS, W), F32)

    def phi_of(n):
        return part[2 * n, 0] + part[2 * n + 1, 0]

    def xi_of(n):
        return part[2 * n, 1] + part[2 * n + 1, 1]

    last = CHIPS - 1
    vs, qs, ps, ws = vq[last, 0], vq[last, 1], phi_of(last), xi_of(last)
    suf_v[last], suf_q[last], suf_w[last] = vs, qs, ws
    pv, pz = vq[0, 0], phi_of(0)
    pre_v[1], pre_z[1] = pv, pz
    for n in reversed(range(last)):
        here = vq[n, 0]
        both = times(jnp.concatenate([here, phi_of(n)], 0), jnp.concatenate([vs, qs], 1))
        vs = both[:W, :W]
        ps = ps + both[W:, :W]
        ahead = jnp.concatenate([both[:W, W:], ws + both[W:, W:]], 0)
        ahead = times_t(ahead, here)
        qs = vq[n, 1] + ahead[:W]
        ws = xi_of(n) + ahead[W:]
        suf_v[n], suf_q[n], suf_w[n] = vs, qs, ws
        up = last - n
        if up < last:
            both = times(jnp.concatenate([pv, pz], 0), vq[up, 0])
            pv, pz = both[:W], both[W:] + phi_of(up)
            pre_v[up + 1], pre_z[up + 1] = pv, pz
    xg[g, :W] = vs
    xg[g, W : 2 * W] = qs
    xg[g, 2 * W : 2 * W + ROWS] = ps
    xg[g, 2 * W + ROWS :] = ws
    x_copies = []
    for k in range(1, 4):
        x_copies.append(send(xg.at[g], xg.at[g], x_ss.at[k - 1], x_rs.at[k - 1], plane_peer(k)))
    for copy in x_copies:
        copy.wait_recv()

    def group(n):
        return xg[n, :W], xg[n, W : 2 * W], xg[n, 2 * W : 2 * W + ROWS], xg[n, 2 * W + ROWS :]

    ga, gb, gc, gd = group(0), group(1), group(2), group(3)
    z1 = ga[2]
    z2 = gb[2] + times(z1, gb[0])
    z3 = gc[2] + times(z2, gc[0])
    w2 = gd[3] + times(z3, gd[1])
    w1 = gc[3] + times(z2, gc[1]) + times_t(w2, gc[0])
    w0 = gb[3] + times(z1, gb[1]) + times_t(w1, gb[0])
    none = jnp.zeros((ROWS, W), F32)
    ends[0, 0], ends[0, 1] = none, w0
    ends[1, 0], ends[1, 1] = z1, w1
    ends[2, 0], ends[2, 1] = z2, w2
    ends[3, 0], ends[3, 1] = z3, none
    z_in = ends[g, 0]
    w_in = ends[g, 1]
    z_chip = pre_z[m] + times(z_in, pre_v[m])
    z_next = part[2 * m, 0] + part[2 * m + 1, 0] + times(z_chip, vm)
    w_chip = suf_w[m + 1] + times(z_next, suf_q[m + 1]) + times_t(w_in, suf_v[m + 1])
    z_even = part[2 * m, 2] + times(z_chip, v0)
    z_odd = part[2 * m + 1, 2] + times(z_even, v1)
    w_even = times_t(z_odd + w_chip, v1)
    x = times(jnp.where(core == 0, z_even + w_even, z_odd + w_chip), dinv)
    xs[u] = x
    fin_copies = []
    for k in range(1, SUBS):
        fin_copies.append(send(xs.at[u], xs.at[u], fin_ss.at[k - 1], fin_rs.at[k - 1], sub_peer(k)))
    for k in range(SUBS):
        v = lax.rem(u + k, SUBS)
        fin_copies.append(send(xs.at[u], xl.at[u], nxt_ss.at[k], nxt_rs.at[k], (after, v)))
    for copy in fin_copies:
        copy.wait_recv()
    own_ref[...] = xs[...].reshape(R, W)
    left_ref[...] = jnp.where(s > 0, xl[...].reshape(R, W), 0.0)

    for copy in [pair_copy] + z_copies + red_copies + ring_copies + f_copies + x_copies + fin_copies:
        copy.wait_send()


def up_kernel(pat, y, own, left, inv_hbm, off_hbm, x_ref, inv, off, known, inv_sem, off_sem):
    inv_copies = {}
    off_copies = {}
    for j in reversed(range(LOC)):
        inv_copies[j] = pltpu.make_async_copy(inv_hbm.at[j], inv.at[j], inv_sem.at[j])
        off_copies[j] = pltpu.make_async_copy(off_hbm.at[j], off.at[j], off_sem.at[j])
        inv_copies[j].start()
        off_copies[j].start()
    known[:LOC] = jnp.zeros_like(y)
    known[LOC] = own[...]
    known[LOC + 1] = left[...]
    for j in reversed(range(LOC)):
        inv_copies[j].wait()
        off_copies[j].wait()
        pulled = y[j]
        for k in range(KB):
            target = pat[k, j]
            weight = jnp.where(target >= 0, 1.0, 0.0).astype(F32)
            pulled = pulled - times(known[jnp.maximum(target, 0)] * weight, off[j, k])
        x = times(pulled, inv[j])
        known[j] = x
        x_ref[j] = x


IN_VMEM = pl.BlockSpec(memory_space=pltpu.VMEM)
IN_SMEM = pl.BlockSpec(memory_space=pltpu.SMEM)
IN_HBM = pl.BlockSpec(memory_space=pltpu.HBM)


def rows_of(*shape):
    return jax.ShapeDtypeStruct(shape, F32)


def shards(rhs_local, diag_inv, off_blocks, pattern, sep_rhs, sep_inv, coupling):
    rhs = rhs_local[0, 0]
    inverse = diag_inv[0, 0]
    blocks = off_blocks[0, 0]
    targets = pattern[0, 0].T
    dma = pltpu.SemaphoreType.DMA
    vmem = pltpu.VMEM
    solved, own, left = pl.pallas_call(
        chain_kernel,
        name="down_and_chain",
        out_shape=(rows_of(LOC, R, W), rows_of(R, W), rows_of(R, W)),
        in_specs=[IN_SMEM] + [IN_HBM] * 6,
        out_specs=(IN_VMEM, IN_VMEM, IN_VMEM),
        scratch_shapes=[
            vmem((LOC, R, W), F32),
            vmem((SUBS, ROWS, W), F32),
            vmem((W, W), F32),
            vmem((W, W), F32),
            dma((4,)),
            vmem((LOC, W, W), F32),
            vmem((LOC, KB, W, W), F32),
            vmem((LOC + 2, SUBS, ROWS, W), F32),
            vmem((2, W, W), F32),
            vmem((CHIPS, 2, W, W), F32),
            vmem((RING, 3, ROWS, W), F32),
            vmem((4, 2 * W + 2 * ROWS, W), F32),
            vmem((SUBS, ROWS, W), F32),
            vmem((SUBS, ROWS, W), F32),
            vmem((SUBS, ROWS, W), F32),
            vmem((SUBS, ROWS, W), F32),
            vmem((CHIPS + 1, W, W), F32),
            vmem((CHIPS + 1, W, W), F32),
            vmem((CHIPS + 1, ROWS, W), F32),
            vmem((CHIPS, W, W), F32),
            vmem((CHIPS, ROWS, W), F32),
            vmem((4, 2, ROWS, W), F32),
            dma((LOC,)), dma((LOC,)),
            dma(()), dma(()),
            dma((7,)), dma((7,)),
            dma((7,)), dma((7,)),
            dma((15,)), dma((15,)),
            dma((3,)), dma((3,)),
            dma((3,)), dma((3,)),
            dma((4,)), dma((4,)),
            dma((3,)), dma((3,)),
            dma((4,)), dma((4,)),
        ],
        compiler_params=pltpu.CompilerParams(
            collective_id=0, has_side_effects=True, vmem_limit_bytes=62 << 20
        ),
    )(targets, rhs, inverse, blocks, sep_rhs[0].reshape(SUBS, ROWS, W), sep_inv[0], coupling[0])
    tree_solution = pl.pallas_call(
        up_kernel,
        name="up",
        out_shape=rows_of(LOC, R, W),
        in_specs=[IN_SMEM, IN_VMEM, IN_VMEM, IN_VMEM, IN_HBM, IN_HBM],
        out_specs=IN_VMEM,
        scratch_shapes=[
            vmem((LOC, W, W), F32),
            vmem((LOC, KB, W, W), F32),
            vmem((LOC + 2, R, W), F32),
            dma((LOC,)),
            dma((LOC,)),
        ],
        compiler_params=pltpu.CompilerParams(vmem_limit_bytes=62 << 20),
    )(targets, solved, own, left, inverse, blocks)
    return tree_solution[None, None], own[None]


def solution(mesh):
    in_specs = (
        P("seg", "sub", None, None, None),
        P("seg", "sub", None, None, None),
        P("seg", "sub", None, None, None, None),
        P("seg", "sub", None, None),
        P("seg", None, None),
        P("seg", None, None),
        P("seg", None, None),
    )
    out_specs = (P("seg", "sub", None, None, None), P("seg", None, None))
    return jax.shard_map(shards, mesh=mesh, in_specs=in_specs, out_specs=out_specs, check_vma=False)
```

```python
import jax
import jax.numpy as jnp
from jax import lax
from jax.experimental import pallas as pl
from jax.experimental.pallas import tpu as pltpu
from jax.sharding import PartitionSpec as P

BF = jnp.bfloat16
F32 = jnp.float32
MESH = pl.DeviceIdType.MESH
LOC, KB, R, W = 16, 4, 32, 128
SEGS, SUBS = 64, 4
RING, CHIPS, ROWS = 16, 8, 8


def halves(v):
    high = v.astype(BF)
    return high, (v - high.astype(F32)).astype(BF)


def left_operand(v):
    high, low = halves(v)
    top = jnp.concatenate([high, high], 1)
    bottom = jnp.concatenate([low, jnp.zeros_like(low)], 1)
    return jnp.concatenate([top, bottom], 0)


def folded(left, right, dims):
    both = lax.dot_general(left, right, (dims, ((), ())), preferred_element_type=F32)
    half = both.shape[0] // 2
    return both[:half] + both[half:]


def times(v, w):
    high, low = halves(w)
    return folded(left_operand(v), jnp.concatenate([high, low], 0), ((1,), (0,)))


def times_t(v, w):
    high, low = halves(w)
    return folded(left_operand(v), jnp.concatenate([high, low], 1), ((1,), (1,)))


def t_times(w, v):
    return times(w.T, v)


def solve_kernel(
    pat, rhs_hbm, inv_hbm, off_hbm, sep_rhs_hbm, sep_inv_hbm, coupling_hbm,
    x_ref, own_ref,
    rhs, sep_rhs, sep_inv, coupling, small_sem,
    inv, off, acc, ys, prev_inv, vpair, vq, part, mine, xg, xr, terms, xs,
    suf_v, suf_q, suf_w, pre_v, pre_z, ends, g_high, g_low, given, known_high, known_low,
    inv_sem, off_sem, prev_ss, prev_rs, pair_ss, pair_rs, z_ss, z_rs, f_ss, f_rs, ring_ss, ring_rs,
    mine_ss, mine_rs, x_ss, x_rs, h_ss, h_rs, r_ss, r_rs, red_ss, red_rs, fin_ss, fin_rs,
):
    s = lax.axis_index("seg")
    u = lax.axis_index("sub")
    core = s % 2
    m = (s // 2) % CHIPS
    i = s % RING
    g = s // RING
    base = s - i
    first_core = core == 0

    def send(src, dst, ss, rs, target):
        copy = pltpu.make_async_remote_copy(
            src_ref=src, dst_ref=dst, send_sem=ss, recv_sem=rs, device_id=target, device_id_type=MESH
        )
        copy.start()
        return copy

    def local(hbm, vmem, sem):
        copy = pltpu.make_async_copy(hbm, vmem, sem)
        copy.start()
        return copy

    sibling = (s + 1 - 2 * core, u)
    after = (lax.rem(s + 1, SEGS), u)
    before = (lax.rem(s + SEGS - 1, SEGS), u)

    def ring_peer(k):
        return (base + lax.rem(i + k, RING), u)

    def chip_peer(k):
        return (base + lax.rem(i + 2 * k, RING), u)

    def plane_peer(k):
        return (lax.rem(s + RING * k, SEGS), u)

    def sub_peer(k):
        return (s, lax.rem(u + k, SUBS))

    barrier = pltpu.get_barrier_semaphore()
    greeted = [ring_peer(k) for k in (8, 7, 9, 6, 10, 5, 11, 4, 12, 3, 13, 2, 14, 1, 15)]
    greeted += [plane_peer(k) for k in (2, 1, 3)]
    greeted += [sub_peer(k) for k in (2, 1, 3)]
    greeted += [after, before]
    for peer in greeted:
        pl.semaphore_signal(barrier, inc=1, device_id=peer, device_id_type=MESH)

    sep_inv_copy = local(sep_inv_hbm, sep_inv, small_sem.at[0])
    coupling_copy = local(coupling_hbm, coupling, small_sem.at[1])
    rhs_copy = local(rhs_hbm, rhs, small_sem.at[2])
    sep_rhs_copy = local(sep_rhs_hbm, sep_rhs, small_sem.at[3])
    inv_copies = []
    off_copies = []
    for j in range(LOC):
        inv_copies.append(local(inv_hbm.at[j], inv.at[j], inv_sem.at[j]))
        off_copies.append(local(off_hbm.at[j], off.at[j], off_sem.at[j]))

    sep_inv_copy.wait()
    coupling_copy.wait()
    dinv = sep_inv[...]
    own_v = -times(dinv, coupling[...]).T
    own_v = jnp.where(s > 0, own_v, 0.0)
    vpair[core] = own_v

    acc[...] = jnp.zeros_like(acc)
    rhs_copy.wait()

    def down(j):
        inv_copies[j].wait()
        off_copies[j].wait()
        y = times_t(rhs[j] - acc[j].reshape(R, W), inv[j])
        ys[j] = y
        products = times_t(y, off[j].reshape(KB * W, W))
        width = LOC + 1 - j
        ids = lax.broadcasted_iota(jnp.int32, (width, 1, ROWS, W), 0) + (j + 1)
        total = acc[j + 1 :]
        for k in range(KB):
            piece = products[:, k * W : (k + 1) * W].reshape(1, SUBS, ROWS, W)
            total = total + jnp.where(ids == pat[k, j], piece, 0.0)
        acc[j + 1 :] = total

    def prepare_up(j):
        stacked = jnp.concatenate([off[j].reshape(KB * W, W), ys[j]], 0)
        both = times(stacked, inv[j])
        high, low = halves(both[: KB * W])
        g_high[j] = high
        g_low[j] = low
        given[j] = both[KB * W :]

    for j in range(0, 8):
        down(j)

    pl.semaphore_wait(barrier, len(greeted))
    pair_copy = send(vpair.at[core], vpair.at[core], pair_ss, pair_rs, sibling)
    prev_copy = send(sep_inv, prev_inv, prev_ss, prev_rs, after)
    for j in range(8, 10):
        down(j)
    pair_copy.wait_recv()
    v0 = vpair[0]
    v1 = vpair[1]
    vm = times(v0, v1)
    vq[m, 0] = vm
    vq[m, 1] = times_t(v0, v0) + times_t(vm, vm)
    z_copies = {}
    f_copies = []

    def z_send(way, step, piece):
        source = lax.rem(m + (CHIPS + 1 - step if way == 0 else step - 1), CHIPS)
        where = vq.at[source, core, pl.ds(piece * (W // 2), W // 2)]
        index = way * 8 + (step - 1) * 2 + piece
        z_copies[way, step, piece] = send(
            where, where, z_ss.at[index], z_rs.at[index], chip_peer(1 if way == 0 else CHIPS - 1)
        )

    def f_send(distance, index):
        where = vq.at[lax.rem(m + CHIPS + distance, CHIPS), core]
        f_copies.append(send(where, where, f_ss.at[index], f_rs.at[index], sibling))

    def z_step(step):
        for piece in range(2):
            for way in range(2):
                z_copies[way, step - 1, piece].wait_recv()
                if step < 4 or way == piece:
                    z_send(way, step, piece)
        f_send(1 - step, step - 2)
        f_send(step - 1, step + 1)

    for piece in range(2):
        for way in range(2):
            z_send(way, 1, piece)
    for j in range(10, LOC):
        down(j)

    red_copies = []
    for k in (2, 1, 3):
        peer = sub_peer(k)
        red_copies.append(
            send(acc.at[pl.ds(LOC, 2), peer[1]], terms.at[u], red_ss.at[k - 1], red_rs.at[k - 1], peer)
        )
    terms[u] = acc[LOC:, u]
    z_step(2)
    for j in range(4):
        prepare_up(j)
    z_step(3)
    for j in range(4, 6):
        prepare_up(j)
    sep_rhs_copy.wait()
    for copy in red_copies:
        copy.wait_recv()
    prev_copy.wait_recv()
    summed = (terms[0] + terms[1]) + (terms[2] + terms[3])
    delta = jnp.where(s > 0, -times_t(summed[1], prev_inv[...]), 0.0)
    phi = times_t(sep_rhs[u] - summed[0], dinv) + times(delta, vpair[core])
    phi_part = jnp.where(first_core, times(phi, v1), phi)
    part[i, 0] = phi_part
    part[i, 1] = (
        times_t(jnp.where(first_core, phi, delta), v0)
        + jnp.where(first_core, delta, 0.0)
        + times_t(phi_part, vm)
    )
    mine[core, 0] = phi
    mine[core, 1] = delta
    ring_copies = []
    for k in (8, 7, 9, 6, 10, 5, 11, 4, 12, 3, 13, 2, 14, 1, 15):
        ring_copies.append(send(part.at[i], part.at[i], ring_ss.at[k - 1], ring_rs.at[k - 1], ring_peer(k)))
    mine_copy = send(mine.at[core], mine.at[core], mine_ss, mine_rs, sibling)

    z_step(4)
    for j in range(6, 9):
        prepare_up(j)
    z_copies[0, 4, 0].wait_recv()
    z_copies[1, 4, 1].wait_recv()
    f_send(4, 6)
    for copy in f_copies:
        copy.wait_recv()

    eye = (
        lax.broadcasted_iota(jnp.int32, (W, W), 0) == lax.broadcasted_iota(jnp.int32, (W, W), 1)
    ).astype(F32)
    suf_v[CHIPS] = eye
    suf_q[CHIPS] = jnp.zeros((W, W), F32)
    suf_w[CHIPS] = jnp.zeros((ROWS, W), F32)
    pre_v[0] = eye
    pre_z[0] = jnp.zeros((ROWS, W), F32)
    last = CHIPS - 1
    vs, qs = vq[last, 0], vq[last, 1]
    suf_v[last], suf_q[last] = vs, qs
    pv = vq[0, 0]
    pre_v[1] = pv
    for n in reversed(range(last)):
        both = times(vq[n, 0], jnp.concatenate([vs, qs], 1))
        vs = both[:, :W]
        qs = vq[n, 1] + times_t(both[:, W:], vq[n, 0])
        suf_v[n], suf_q[n] = vs, qs
        up = last - n
        if up < last:
            pv = times(pv, vq[up, 0])
            pre_v[up + 1] = pv
    xg[g, 0] = vs
    xg[g, 1] = qs
    x_copies = []
    for k in (2, 1, 3):
        x_copies.append(send(xg.at[g, core], xg.at[g, core], x_ss.at[k - 1], x_rs.at[k - 1], plane_peer(k)))

    mine_copy.wait_recv()
    for copy in ring_copies:
        copy.wait_recv()

    phis = [part[2 * n, 0] + part[2 * n + 1, 0] for n in range(CHIPS)]
    xis = [part[2 * n, 1] + part[2 * n + 1, 1] for n in range(CHIPS)]
    ps, ws, pz = phis[last], xis[last], phis[0]
    suf_w[last] = ws
    pre_z[1] = pz
    for n in reversed(range(last)):
        ps = ps + times(phis[n], suf_v[n + 1])
        ws = xis[n] + times_t(ws + times(phis[n], suf_q[n + 1]), vq[n, 0])
        suf_w[n] = ws
        up = last - n
        if up < last:
            pz = phis[up] + times(pz, vq[up, 0])
            pre_z[up + 1] = pz
    xr[g, 0] = ps
    xr[g, 1] = ws
    r_copies = []
    for k in (2, 1, 3):
        r_copies.append(send(xr.at[g], xr.at[g], r_ss.at[k - 1], r_rs.at[k - 1], plane_peer(k)))
    known_high[...] = jnp.zeros_like(known_high)
    known_low[...] = jnp.zeros_like(known_low)
    h_copies = []
    for k in (1, 3, 2):
        x_copies[(2, 1, 3).index(k)].wait_recv()
        source = lax.rem(g + 4 - k, 4)
        h_copies.append(
            send(xg.at[source, core], xg.at[source, core], h_ss.at[k - 1], h_rs.at[k - 1], sibling)
        )
    for j in range(9, LOC):
        prepare_up(j)
    for copy in h_copies + r_copies:
        copy.wait_recv()

    def group(n):
        return xg[n, 0], xg[n, 1], xr[n, 0], xr[n, 1]

    ga, gb, gc, gd = group(0), group(1), group(2), group(3)
    z1 = ga[2]
    z2 = gb[2] + times(z1, gb[0])
    z3 = gc[2] + times(z2, gc[0])
    w2 = gd[3] + times(z3, gd[1])
    w1 = gc[3] + times(z2, gc[1]) + times_t(w2, gc[0])
    w0 = gb[3] + times(z1, gb[1]) + times_t(w1, gb[0])
    none = jnp.zeros((ROWS, W), F32)
    ends[0, 0], ends[0, 1] = none, w0
    ends[1, 0], ends[1, 1] = z1, w1
    ends[2, 0], ends[2, 1] = z2, w2
    ends[3, 0], ends[3, 1] = z3, none
    z_in = ends[g, 0]
    w_in = ends[g, 1]
    z_chip = pre_z[m] + times(z_in, pre_v[m])
    z_next = part[2 * m, 0] + part[2 * m + 1, 0] + times(z_chip, vm)
    w_chip = suf_w[m + 1] + times(z_next, suf_q[m + 1]) + times_t(w_in, suf_v[m + 1])
    z_even = mine[0, 0] + times(z_chip, v0)
    odd = mine[1, 0] + times(z_even, v1) + w_chip
    even = z_even + times_t(odd, v1) + mine[1, 1]
    outer = z_chip + times_t(even, v0) + mine[0, 1]
    xs[u, 0] = times(jnp.where(first_core, even, odd), dinv)
    xs[u, 1] = jnp.where(s > 0, times(jnp.where(first_core, outer, even), prev_inv[...]), 0.0)
    fin_copies = []
    for k in (2, 1, 3):
        fin_copies.append(send(xs.at[u], xs.at[u], fin_ss.at[k - 1], fin_rs.at[k - 1], sub_peer(k)))
    for copy in fin_copies:
        copy.wait_recv()

    def learn(t, x):
        high, low = halves(x)
        known_high[t] = high
        known_low[t] = low

    own = jnp.concatenate([xs[v, 0] for v in range(SUBS)], 0)
    own_ref[...] = own
    learn(LOC, own)
    learn(LOC + 1, jnp.concatenate([xs[v, 1] for v in range(SUBS)], 0))
    for j in reversed(range(LOC)):
        places = []
        for k in range(KB):
            target = pat[k, j]
            places.append(jnp.where(target >= 0, target, LOC + 2))
        high = jnp.concatenate([known_high[t] for t in places], 1)
        low = jnp.concatenate([known_low[t] for t in places], 1)
        pulled = folded(jnp.concatenate([high, low], 0), g_high[j], ((1,), (0,)))
        pulled += jnp.dot(high, g_low[j], preferred_element_type=F32)
        x = given[j] - pulled
        learn(j, x)
        x_ref[j] = x

    started = [pair_copy, prev_copy, mine_copy] + list(z_copies.values()) + red_copies + ring_copies + r_copies
    for copy in started + f_copies + x_copies + h_copies + fin_copies:
        copy.wait_send()


def store_kernel(x, own, x_out, own_out, x_sem, own_sem):
    x_copy = pltpu.make_async_copy(x, x_out, x_sem)
    own_copy = pltpu.make_async_copy(own, own_out, own_sem)
    x_copy.start()
    own_copy.start()
    x_copy.wait()
    own_copy.wait()


IN_VMEM = pl.BlockSpec(memory_space=pltpu.VMEM)
IN_SMEM = pl.BlockSpec(memory_space=pltpu.SMEM)
IN_HBM = pl.BlockSpec(memory_space=pltpu.HBM)


def rows_of(*shape):
    return jax.ShapeDtypeStruct(shape, F32)


def shards(rhs_local, diag_inv, off_blocks, pattern, sep_rhs, sep_inv, coupling):
    rhs = rhs_local[0, 0]
    inverse = diag_inv[0, 0]
    blocks = off_blocks[0, 0]
    targets = pattern[0, 0].T
    dma = pltpu.SemaphoreType.DMA
    vmem = pltpu.VMEM
    tree_solution, own = pl.pallas_call(
        solve_kernel,
        name="solve",
        out_shape=(rows_of(LOC, R, W), rows_of(R, W)),
        in_specs=[IN_SMEM] + [IN_HBM] * 6,
        out_specs=(IN_VMEM, IN_VMEM),
        scratch_shapes=[
            vmem((LOC, R, W), F32),
            vmem((SUBS, ROWS, W), F32),
            vmem((W, W), F32),
            vmem((W, W), F32),
            dma((4,)),
            vmem((LOC, W, W), F32),
            vmem((LOC, KB, W, W), F32),
            vmem((LOC + 2, SUBS, ROWS, W), F32),
            vmem((LOC, R, W), F32),
            vmem((W, W), F32),
            vmem((2, W, W), F32),
            vmem((CHIPS, 2, W, W), F32),
            vmem((RING, 2, ROWS, W), F32),
            vmem((2, 2, ROWS, W), F32),
            vmem((4, 2, W, W), F32),
            vmem((4, 2, ROWS, W), F32),
            vmem((SUBS, 2, ROWS, W), F32),
            vmem((SUBS, 2, ROWS, W), F32),
            vmem((CHIPS + 1, W, W), F32),
            vmem((CHIPS + 1, W, W), F32),
            vmem((CHIPS + 1, ROWS, W), F32),
            vmem((CHIPS, W, W), F32),
            vmem((CHIPS, ROWS, W), F32),
            vmem((4, 2, ROWS, W), F32),
            vmem((LOC, KB * W, W), BF),
            vmem((LOC, KB * W, W), BF),
            vmem((LOC, R, W), F32),
            vmem((LOC + 3, R, W), BF),
            vmem((LOC + 3, R, W), BF),
            dma((LOC,)), dma((LOC,)),
            dma(()), dma(()),
            dma(()), dma(()),
            dma((16,)), dma((16,)),
            dma((7,)), dma((7,)),
            dma((15,)), dma((15,)),
            dma(()), dma(()),
            dma((3,)), dma((3,)),
            dma((3,)), dma((3,)),
            dma((3,)), dma((3,)),
            dma((3,)), dma((3,)),
            dma((3,)), dma((3,)),
        ],
        compiler_params=pltpu.CompilerParams(
            collective_id=0, has_side_effects=True, vmem_limit_bytes=62 << 20
        ),
    )(targets, rhs, inverse, blocks, sep_rhs[0].reshape(SUBS, ROWS, W), sep_inv[0], coupling[0])
    tree_solution, own = pl.pallas_call(
        store_kernel,
        name="store",
        out_shape=(rows_of(LOC, R, W), rows_of(R, W)),
        in_specs=[IN_VMEM, IN_VMEM],
        out_specs=(IN_HBM, IN_HBM),
        scratch_shapes=[dma(()), dma(())],
    )(tree_solution, own)
    return tree_solution[None, None], own[None]


def solution(mesh):
    in_specs = (
        P("seg", "sub", None, None, None),
        P("seg", "sub", None, None, None),
        P("seg", "sub", None, None, None, None),
        P("seg", "sub", None, None),
        P("seg", None, None),
        P("seg", None, None),
        P("seg", None, None),
    )
    out_specs = (P("seg", "sub", None, None, None), P("seg", None, None))
    return jax.shard_map(shards, mesh=mesh, in_specs=in_specs, out_specs=out_specs, check_vma=False)
```

```python
import jax
import jax.numpy as jnp
from jax import lax
from jax.experimental import pallas as pl
from jax.experimental.pallas import tpu as pltpu
from jax.sharding import PartitionSpec as P

BF = jnp.bfloat16
F32 = jnp.float32
MESH = pl.DeviceIdType.MESH
LOC, KB, R, W = 16, 4, 32, 128
SEGS, SUBS = 64, 4
RING, CHIPS, ROWS = 16, 8, 8


def halves(v):
    high = v.astype(BF)
    return high, (v - high.astype(F32)).astype(BF)


def left_operand(v):
    high, low = halves(v)
    top = jnp.concatenate([high, high], 1)
    bottom = jnp.concatenate([low, jnp.zeros_like(low)], 1)
    return jnp.concatenate([top, bottom], 0)


def folded(left, right, dims):
    both = lax.dot_general(left, right, (dims, ((), ())), preferred_element_type=F32)
    half = both.shape[0] // 2
    return both[:half] + both[half:]


def times(v, w):
    high, low = halves(w)
    return folded(left_operand(v), jnp.concatenate([high, low], 0), ((1,), (0,)))


def times_t(v, w):
    high, low = halves(w)
    return folded(left_operand(v), jnp.concatenate([high, low], 1), ((1,), (1,)))


def t_times(w, v):
    return times(w.T, v)


def solve_kernel(
    pat, rhs_hbm, inv_hbm, off_hbm, sep_rhs_hbm, sep_inv_hbm, coupling_hbm,
    x_ref, own_ref,
    rhs, sep_rhs, sep_inv, coupling, small_sem,
    inv, off, acc, ys, prev_inv, vr, vq, part, mine, xg, xr, terms, xs,
    suf_v, suf_q, suf_w, pre_v, pre_z, ends, g_high, g_low, given, known_high, known_low,
    inv_sem, off_sem, prev_ss, prev_rs, relays, z_ss, z_rs, f_ss, f_rs, ring_ss, ring_rs,
    mine_ss, mine_rs, x_ss, x_rs, h_ss, h_rs, r_ss, r_rs, red_ss, red_rs, fin_ss, fin_rs,
):
    s = lax.axis_index("seg")
    u = lax.axis_index("sub")
    core = s % 2
    m = (s // 2) % CHIPS
    i = s % RING
    g = s // RING
    base = s - i
    first_core = core == 0

    def send(src, dst, ss, rs, target):
        copy = pltpu.make_async_remote_copy(
            src_ref=src, dst_ref=dst, send_sem=ss, recv_sem=rs, device_id=target, device_id_type=MESH
        )
        copy.start()
        return copy

    def local(hbm, vmem, sem):
        copy = pltpu.make_async_copy(hbm, vmem, sem)
        copy.start()
        return copy

    sibling = (s + 1 - 2 * core, u)
    after = (lax.rem(s + 1, SEGS), u)
    before = (lax.rem(s + SEGS - 1, SEGS), u)

    def chip_peer(k):
        return (base + lax.rem(i + 2 * k, RING), u)

    def plane_peer(k):
        return (lax.rem(s + RING * k, SEGS), u)

    def sub_peer(k):
        return (s, lax.rem(u + k, SUBS))

    barrier = pltpu.get_barrier_semaphore()
    far_first = (4, 3, 5, 2, 6, 1, 7)
    chip_sides = (chip_peer(1), chip_peer(CHIPS - 1))
    greeted = [after, before, sibling, *chip_sides]
    greeted += [plane_peer(1), plane_peer(3), sub_peer(1), sub_peer(3)]
    for peer in greeted:
        pl.semaphore_signal(barrier, inc=1, device_id=peer, device_id_type=MESH)

    rhs_copy = local(rhs_hbm, rhs, small_sem.at[2])
    tree_copies = {}
    for n, (low, high) in enumerate(((0, 1), (1, 2), (2, 4), (4, 8), (8, 16))):
        run = pl.ds(low, high - low)
        tree_copies[low] = (
            local(inv_hbm.at[run], inv.at[run], inv_sem.at[n]),
            local(off_hbm.at[run], off.at[run], off_sem.at[n]),
        )
        if n == 1:
            sep_inv_copy = local(sep_inv_hbm, sep_inv, small_sem.at[0])
            coupling_copy = local(coupling_hbm, coupling, small_sem.at[1])
    sep_rhs_copy = local(sep_rhs_hbm, sep_rhs, small_sem.at[3])

    acc[...] = jnp.zeros_like(acc)
    rhs_copy.wait()

    def down(j):
        for copy in tree_copies.get(j, ()):
            copy.wait()
        y = times_t(rhs[j] - acc[j].reshape(R, W), inv[j])
        ys[j] = y
        products = times_t(y, off[j].reshape(KB * W, W))
        width = LOC + 1 - j
        ids = lax.broadcasted_iota(jnp.int32, (width, 1, ROWS, W), 0) + (j + 1)
        total = acc[j + 1 :]
        for k in range(KB):
            piece = products[:, k * W : (k + 1) * W].reshape(1, SUBS, ROWS, W)
            total = total + jnp.where(ids == pat[k, j], piece, 0.0)
        acc[j + 1 :] = total

    def prepare_up(j):
        stacked = jnp.concatenate([off[j].reshape(KB * W, W), ys[j]], 0)
        both = times(stacked, inv[j])
        high, low = halves(both[: KB * W])
        g_high[j] = high
        g_low[j] = low
        given[j] = both[KB * W :]

    z_copies = {}
    f_copies = {}

    def chip_at(distance):
        return lax.rem(m + CHIPS + distance, CHIPS)

    def z_send(way, step, piece):
        source = 2 * chip_at(1 - step if way == 0 else step - 1) + core
        where = vr.at[source, pl.ds(piece * (W // 2), W // 2)]
        index = way * 8 + (step - 1) * 2 + piece
        z_copies[way, step, piece] = send(where, where, z_ss.at[index], z_rs.at[index], chip_sides[way])

    def f_send(distance, index):
        where = vr.at[2 * chip_at(distance) + core]
        f_copies[distance] = send(where, where, f_ss.at[index], f_rs.at[index], sibling)

    def z_step(step):
        for piece in range(2):
            for way in range(2):
                z_copies[way, step - 1, piece].wait_recv()
                if step < 4 or way == piece:
                    z_send(way, step, piece)
        f_send(1 - step, step - 2)
        f_send(step - 1, step + 1)

    def merge(distance):
        f_copies[distance].wait_recv()
        chip = chip_at(distance)
        first, second = vr[2 * chip], vr[2 * chip + 1]
        pair = times(first, second)
        vq[chip, 0] = pair
        vq[chip, 1] = times_t(first, first) + times_t(pair, pair)

    def relay(level, peers):
        for peer in peers:
            pl.semaphore_signal(relays.at[level], inc=1, device_id=peer, device_id_type=MESH)

    down(0)
    sep_inv_copy.wait()
    coupling_copy.wait()
    dinv = sep_inv[...]
    own_v = -times(dinv, coupling[...]).T
    own_v = jnp.where(s > 0, own_v, 0.0)
    vr[i] = own_v
    down(1)

    pl.semaphore_wait(barrier, len(greeted))
    for piece in range(2):
        for way in range(2):
            z_send(way, 1, piece)
    f_send(0, 7)
    prev_copy = send(sep_inv, prev_inv, prev_ss, prev_rs, after)
    relay(0, [*chip_sides, plane_peer(3), sub_peer(3)])
    for j in range(2, 6):
        down(j)
    pl.semaphore_wait(relays.at[0], 4)
    relay(1, chip_sides)
    for j in range(6, 9):
        down(j)
    z_step(2)
    for j in range(9, 11):
        down(j)
    pl.semaphore_wait(relays.at[1], 2)
    relay(2, chip_sides)
    for j in range(11, LOC):
        down(j)

    red_copies = []
    for k in (2, 1, 3):
        peer = sub_peer(k)
        red_copies.append(
            send(acc.at[pl.ds(LOC, 2), peer[1]], terms.at[u], red_ss.at[k - 1], red_rs.at[k - 1], peer)
        )
    terms[u] = acc[LOC:, u]
    z_step(3)
    merge(0)
    v0 = vr[2 * m]
    v1 = vr[2 * m + 1]
    vm = vq[m, 0]
    merge(-1)
    merge(1)
    for j in range(0, 4):
        prepare_up(j)
    pl.semaphore_wait(relays.at[2], 2)
    sep_rhs_copy.wait()
    for copy in red_copies:
        copy.wait_recv()
    prev_copy.wait_recv()
    summed = (terms[0] + terms[1]) + (terms[2] + terms[3])
    delta = jnp.where(s > 0, -times_t(summed[1], prev_inv[...]), 0.0)
    phi = times_t(sep_rhs[u] - summed[0], dinv) + times(delta, vr[i])
    mine[core, 0] = phi
    mine[core, 1] = delta
    mine_copy = send(mine.at[core], mine.at[core], mine_ss, mine_rs, sibling)
    mine_copy.wait_recv()
    phi_chip = mine[1, 0] + times(mine[0, 0], v1)
    part[m, 0] = phi_chip
    part[m, 1] = times_t(mine[0, 0] + mine[1, 1], v0) + mine[0, 1] + times_t(phi_chip, vm)
    ring_copies = []
    for k in far_first:
        ring_copies.append(send(part.at[m], part.at[m], ring_ss.at[k - 1], ring_rs.at[k - 1], chip_peer(k)))

    z_step(4)
    merge(-2)
    merge(2)
    for j in range(4, 6):
        prepare_up(j)
    z_copies[0, 4, 0].wait_recv()
    z_copies[1, 4, 1].wait_recv()
    f_send(4, 6)
    merge(-3)
    merge(3)
    merge(4)

    eye = (
        lax.broadcasted_iota(jnp.int32, (W, W), 0) == lax.broadcasted_iota(jnp.int32, (W, W), 1)
    ).astype(F32)
    suf_v[CHIPS] = eye
    suf_q[CHIPS] = jnp.zeros((W, W), F32)
    suf_w[CHIPS] = jnp.zeros((ROWS, W), F32)
    pre_v[0] = eye
    pre_z[0] = jnp.zeros((ROWS, W), F32)
    last = CHIPS - 1
    vs, qs = vq[last, 0], vq[last, 1]
    suf_v[last], suf_q[last] = vs, qs
    pv = vq[0, 0]
    pre_v[1] = pv
    for n in reversed(range(last)):
        both = times(vq[n, 0], jnp.concatenate([vs, qs], 1))
        vs = both[:, :W]
        qs = vq[n, 1] + times_t(both[:, W:], vq[n, 0])
        suf_v[n], suf_q[n] = vs, qs
        up = last - n
        if up < last:
            pv = times(pv, vq[up, 0])
            pre_v[up + 1] = pv
    xg[g, 0] = vs
    xg[g, 1] = qs
    x_copies = []
    for k in (2, 1, 3):
        x_copies.append(send(xg.at[g, core], xg.at[g, core], x_ss.at[k - 1], x_rs.at[k - 1], plane_peer(k)))

    for copy in ring_copies:
        copy.wait_recv()

    phis = [part[n, 0] for n in range(CHIPS)]
    xis = [part[n, 1] for n in range(CHIPS)]
    ps, ws, pz = phis[last], xis[last], phis[0]
    suf_w[last] = ws
    pre_z[1] = pz
    for n in reversed(range(last)):
        ps = ps + times(phis[n], suf_v[n + 1])
        ws = xis[n] + times_t(ws + times(phis[n], suf_q[n + 1]), vq[n, 0])
        suf_w[n] = ws
        up = last - n
        if up < last:
            pz = phis[up] + times(pz, vq[up, 0])
            pre_z[up + 1] = pz
    xr[g, 0] = ps
    xr[g, 1] = ws
    r_copies = []
    for k in (2, 1, 3):
        r_copies.append(send(xr.at[g], xr.at[g], r_ss.at[k - 1], r_rs.at[k - 1], plane_peer(k)))
    known_high[...] = jnp.zeros_like(known_high)
    known_low[...] = jnp.zeros_like(known_low)
    h_copies = []
    for k in (1, 3, 2):
        x_copies[(2, 1, 3).index(k)].wait_recv()
        source = lax.rem(g + 4 - k, 4)
        h_copies.append(
            send(xg.at[source, core], xg.at[source, core], h_ss.at[k - 1], h_rs.at[k - 1], sibling)
        )
    for j in range(6, LOC):
        prepare_up(j)
    for copy in h_copies + r_copies:
        copy.wait_recv()

    def group(n):
        return xg[n, 0], xg[n, 1], xr[n, 0], xr[n, 1]

    ga, gb, gc, gd = group(0), group(1), group(2), group(3)
    z1 = ga[2]
    z2 = gb[2] + times(z1, gb[0])
    z3 = gc[2] + times(z2, gc[0])
    w2 = gd[3] + times(z3, gd[1])
    w1 = gc[3] + times(z2, gc[1]) + times_t(w2, gc[0])
    w0 = gb[3] + times(z1, gb[1]) + times_t(w1, gb[0])
    none = jnp.zeros((ROWS, W), F32)
    ends[0, 0], ends[0, 1] = none, w0
    ends[1, 0], ends[1, 1] = z1, w1
    ends[2, 0], ends[2, 1] = z2, w2
    ends[3, 0], ends[3, 1] = z3, none
    z_in = ends[g, 0]
    w_in = ends[g, 1]
    z_chip = pre_z[m] + times(z_in, pre_v[m])
    z_next = part[m, 0] + times(z_chip, vm)
    w_chip = suf_w[m + 1] + times(z_next, suf_q[m + 1]) + times_t(w_in, suf_v[m + 1])
    z_even = mine[0, 0] + times(z_chip, v0)
    odd = mine[1, 0] + times(z_even, v1) + w_chip
    even = z_even + times_t(odd, v1) + mine[1, 1]
    outer = z_chip + times_t(even, v0) + mine[0, 1]
    xs[u, 0] = times(jnp.where(first_core, even, odd), dinv)
    xs[u, 1] = jnp.where(s > 0, times(jnp.where(first_core, outer, even), prev_inv[...]), 0.0)
    fin_copies = []
    for k in (2, 1, 3):
        fin_copies.append(send(xs.at[u], xs.at[u], fin_ss.at[k - 1], fin_rs.at[k - 1], sub_peer(k)))
    for copy in fin_copies:
        copy.wait_recv()

    def learn(t, x):
        high, low = halves(x)
        known_high[t] = high
        known_low[t] = low

    own = jnp.concatenate([xs[v, 0] for v in range(SUBS)], 0)
    own_ref[...] = own
    learn(LOC, own)
    learn(LOC + 1, jnp.concatenate([xs[v, 1] for v in range(SUBS)], 0))
    for j in reversed(range(LOC)):
        places = []
        for k in range(KB):
            target = pat[k, j]
            places.append(jnp.where(target >= 0, target, LOC + 2))
        high = jnp.concatenate([known_high[t] for t in places], 1)
        low = jnp.concatenate([known_low[t] for t in places], 1)
        pulled = folded(jnp.concatenate([high, low], 0), g_high[j], ((1,), (0,)))
        pulled += jnp.dot(high, g_low[j], preferred_element_type=F32)
        x = given[j] - pulled
        learn(j, x)
        x_ref[j] = x

    started = [prev_copy, mine_copy] + list(z_copies.values()) + list(f_copies.values()) + red_copies + ring_copies + r_copies
    for copy in started + x_copies + h_copies + fin_copies:
        copy.wait_send()


def store_kernel(x, own, x_out, own_out, x_sem, own_sem):
    x_copy = pltpu.make_async_copy(x, x_out, x_sem)
    own_copy = pltpu.make_async_copy(own, own_out, own_sem)
    x_copy.start()
    own_copy.start()
    x_copy.wait()
    own_copy.wait()


IN_VMEM = pl.BlockSpec(memory_space=pltpu.VMEM)
IN_SMEM = pl.BlockSpec(memory_space=pltpu.SMEM)
IN_HBM = pl.BlockSpec(memory_space=pltpu.HBM)


def rows_of(*shape):
    return jax.ShapeDtypeStruct(shape, F32)


def shards(rhs_local, diag_inv, off_blocks, pattern, sep_rhs, sep_inv, coupling):
    rhs = rhs_local[0, 0]
    inverse = diag_inv[0, 0]
    blocks = off_blocks[0, 0]
    targets = pattern[0, 0].T
    dma = pltpu.SemaphoreType.DMA
    vmem = pltpu.VMEM
    tree_solution, own = pl.pallas_call(
        solve_kernel,
        name="solve",
        out_shape=(rows_of(LOC, R, W), rows_of(R, W)),
        in_specs=[IN_SMEM] + [IN_HBM] * 6,
        out_specs=(IN_VMEM, IN_VMEM),
        scratch_shapes=[
            vmem((LOC, R, W), F32),
            vmem((SUBS, ROWS, W), F32),
            vmem((W, W), F32),
            vmem((W, W), F32),
            dma((4,)),
            vmem((LOC, W, W), F32),
            vmem((LOC, KB, W, W), F32),
            vmem((LOC + 2, SUBS, ROWS, W), F32),
            vmem((LOC, R, W), F32),
            vmem((W, W), F32),
            vmem((RING, W, W), F32),
            vmem((CHIPS, 2, W, W), F32),
            vmem((CHIPS, 2, ROWS, W), F32),
            vmem((2, 2, ROWS, W), F32),
            vmem((4, 2, W, W), F32),
            vmem((4, 2, ROWS, W), F32),
            vmem((SUBS, 2, ROWS, W), F32),
            vmem((SUBS, 2, ROWS, W), F32),
            vmem((CHIPS + 1, W, W), F32),
            vmem((CHIPS + 1, W, W), F32),
            vmem((CHIPS + 1, ROWS, W), F32),
            vmem((CHIPS, W, W), F32),
            vmem((CHIPS, ROWS, W), F32),
            vmem((4, 2, ROWS, W), F32),
            vmem((LOC, KB * W, W), BF),
            vmem((LOC, KB * W, W), BF),
            vmem((LOC, R, W), F32),
            vmem((LOC + 3, R, W), BF),
            vmem((LOC + 3, R, W), BF),
            dma((5,)), dma((5,)),
            dma(()), dma(()),
            pltpu.SemaphoreType.REGULAR((3,)),
            dma((16,)), dma((16,)),
            dma((8,)), dma((8,)),
            dma((7,)), dma((7,)),
            dma(()), dma(()),
            dma((3,)), dma((3,)),
            dma((3,)), dma((3,)),
            dma((3,)), dma((3,)),
            dma((3,)), dma((3,)),
            dma((3,)), dma((3,)),
        ],
        compiler_params=pltpu.CompilerParams(
            collective_id=0, has_side_effects=True, vmem_limit_bytes=62 << 20
        ),
    )(targets, rhs, inverse, blocks, sep_rhs[0].reshape(SUBS, ROWS, W), sep_inv[0], coupling[0])
    tree_solution, own = pl.pallas_call(
        store_kernel,
        name="store",
        out_shape=(rows_of(LOC, R, W), rows_of(R, W)),
        in_specs=[IN_VMEM, IN_VMEM],
        out_specs=(IN_HBM, IN_HBM),
        scratch_shapes=[dma(()), dma(())],
    )(tree_solution, own)
    return tree_solution[None, None], own[None]


def solution(mesh):
    in_specs = (
        P("seg", "sub", None, None, None),
        P("seg", "sub", None, None, None),
        P("seg", "sub", None, None, None, None),
        P("seg", "sub", None, None),
        P("seg", None, None),
        P("seg", None, None),
        P("seg", None, None),
    )
    out_specs = (P("seg", "sub", None, None, None), P("seg", None, None))
    return jax.shard_map(shards, mesh=mesh, in_specs=in_specs, out_specs=out_specs, check_vma=False)
```

```python
import jax
import jax.numpy as jnp
from jax import lax
from jax.experimental import pallas as pl
from jax.experimental.pallas import tpu as pltpu
from jax.sharding import PartitionSpec as P

BF = jnp.bfloat16
F32 = jnp.float32
MESH = pl.DeviceIdType.MESH
LOC, KB, R, W = 16, 4, 32, 128
SEGS, SUBS = 64, 4
RING, CHIPS, ROWS = 16, 8, 8


def halves(v):
    high = v.astype(BF)
    return high, (v - high.astype(F32)).astype(BF)


def left_operand(v):
    high, low = halves(v)
    top = jnp.concatenate([high, high], 1)
    bottom = jnp.concatenate([low, jnp.zeros_like(low)], 1)
    return jnp.concatenate([top, bottom], 0)


def folded(left, right, dims):
    both = lax.dot_general(left, right, (dims, ((), ())), preferred_element_type=F32)
    half = both.shape[0] // 2
    return both[:half] + both[half:]


def times(v, w):
    high, low = halves(w)
    return folded(left_operand(v), jnp.concatenate([high, low], 0), ((1,), (0,)))


def times_t(v, w):
    high, low = halves(w)
    return folded(left_operand(v), jnp.concatenate([high, low], 1), ((1,), (1,)))


def t_times(w, v):
    return times(w.T, v)


def solve_kernel(
    pat, rhs_hbm, inv_hbm, off_hbm, sep_rhs_hbm, sep_inv_hbm, coupling_hbm,
    x_ref, own_ref,
    rhs, sep_rhs, sep_inv, coupling, small_sem,
    inv, off, acc, ys, prev_inv, vr, vq, part, mine, xg, xr, terms, xs,
    suf_v, suf_q, suf_w, pre_v, pre_z, ends, g_high, g_low, given, known_high, known_low,
    inv_sem, off_sem, prev_ss, prev_rs, relays, z_ss, z_rs, f_ss, f_rs, ring_ss, ring_rs,
    mine_ss, mine_rs, x_ss, x_rs, h_ss, h_rs, r_ss, r_rs, red_ss, red_rs, fin_ss, fin_rs,
):
    s = lax.axis_index("seg")
    u = lax.axis_index("sub")
    core = s % 2
    m = (s // 2) % CHIPS
    i = s % RING
    g = s // RING
    base = s - i
    first_core = core == 0

    def send(src, dst, ss, rs, target):
        copy = pltpu.make_async_remote_copy(
            src_ref=src, dst_ref=dst, send_sem=ss, recv_sem=rs, device_id=target, device_id_type=MESH
        )
        copy.start()
        return copy

    def local(hbm, vmem, sem):
        copy = pltpu.make_async_copy(hbm, vmem, sem)
        copy.start()
        return copy

    sibling = (s + 1 - 2 * core, u)
    after = (lax.rem(s + 1, SEGS), u)
    before = (lax.rem(s + SEGS - 1, SEGS), u)

    def chip_peer(k):
        return (base + lax.rem(i + 2 * k, RING), u)

    def plane_peer(k):
        return (lax.rem(s + RING * k, SEGS), u)

    def sub_peer(k):
        return (s, lax.rem(u + k, SUBS))

    barrier = pltpu.get_barrier_semaphore()
    far_first = (4, 3, 5, 2, 6, 1, 7)
    chip_sides = (chip_peer(1), chip_peer(CHIPS - 1))
    greeted = [after, before, sibling, *chip_sides]
    greeted += [plane_peer(1), plane_peer(3), sub_peer(1), sub_peer(3)]
    for peer in greeted:
        pl.semaphore_signal(barrier, inc=1, device_id=peer, device_id_type=MESH)

    rhs_copy = local(rhs_hbm, rhs, small_sem.at[2])
    tree_copies = {}
    for n, (low, high) in enumerate(((0, 1), (1, 2), (2, 4), (4, 8), (8, 16))):
        run = pl.ds(low, high - low)
        tree_copies[low] = (
            local(inv_hbm.at[run], inv.at[run], inv_sem.at[n]),
            local(off_hbm.at[run], off.at[run], off_sem.at[n]),
        )
        if n == 1:
            sep_inv_copy = local(sep_inv_hbm, sep_inv, small_sem.at[0])
            coupling_copy = local(coupling_hbm, coupling, small_sem.at[1])
    sep_rhs_copy = local(sep_rhs_hbm, sep_rhs, small_sem.at[3])

    acc[...] = jnp.zeros_like(acc)
    rhs_copy.wait()

    def down(j):
        for copy in tree_copies.get(j, ()):
            copy.wait()
        y = times_t(rhs[j] - acc[j].reshape(R, W), inv[j])
        ys[j] = y
        products = times_t(y, off[j].reshape(KB * W, W))
        width = LOC + 1 - j
        ids = lax.broadcasted_iota(jnp.int32, (width, 1, ROWS, W), 0) + (j + 1)
        total = acc[j + 1 :]
        for k in range(KB):
            piece = products[:, k * W : (k + 1) * W].reshape(1, SUBS, ROWS, W)
            total = total + jnp.where(ids == pat[k, j], piece, 0.0)
        acc[j + 1 :] = total

    def prepare_up(j):
        stacked = jnp.concatenate([off[j].reshape(KB * W, W), ys[j]], 0)
        both = times(stacked, inv[j])
        high, low = halves(both[: KB * W])
        g_high[j] = high
        g_low[j] = low
        given[j] = both[KB * W :]

    z_copies = {}
    f_copies = {}

    def chip_at(distance):
        return lax.rem(m + CHIPS + distance, CHIPS)

    def z_send(way, step, piece):
        source = 2 * chip_at(1 - step if way == 0 else step - 1) + core
        where = vr.at[source, pl.ds(piece * (W // 2), W // 2)]
        index = way * 8 + (step - 1) * 2 + piece
        z_copies[way, step, piece] = send(where, where, z_ss.at[index], z_rs.at[index], chip_sides[way])

    def f_send(distance, index):
        where = vr.at[2 * chip_at(distance) + core]
        f_copies[distance] = send(where, where, f_ss.at[index], f_rs.at[index], sibling)

    def z_step(step):
        for piece in range(2):
            for way in range(2):
                z_copies[way, step - 1, piece].wait_recv()
                if step < 4 or way == piece:
                    z_send(way, step, piece)
        f_send(1 - step, step - 2)
        f_send(step - 1, step + 1)

    def merge(distance):
        f_copies[distance].wait_recv()
        chip = chip_at(distance)
        first, second = vr[2 * chip], vr[2 * chip + 1]
        pair = times(first, second)
        vq[chip, 0] = pair
        vq[chip, 1] = times_t(first, first) + times_t(pair, pair)

    def relay(level, peers):
        for peer in peers:
            pl.semaphore_signal(relays.at[level], inc=1, device_id=peer, device_id_type=MESH)

    down(0)
    sep_inv_copy.wait()
    coupling_copy.wait()
    dinv = sep_inv[...]
    own_v = -times(dinv, coupling[...]).T
    own_v = jnp.where(s > 0, own_v, 0.0)
    vr[i] = own_v
    down(1)

    pl.semaphore_wait(barrier, len(greeted))
    for piece in range(2):
        for way in range(2):
            z_send(way, 1, piece)
    f_send(0, 7)
    prev_copy = send(sep_inv, prev_inv, prev_ss, prev_rs, after)
    relay(0, [*chip_sides, plane_peer(3), sub_peer(3)])
    for j in range(2, 6):
        down(j)
    pl.semaphore_wait(relays.at[0], 4)
    relay(1, chip_sides)
    for j in range(6, 9):
        down(j)
    z_step(2)
    for j in range(9, 11):
        down(j)
    pl.semaphore_wait(relays.at[1], 2)
    relay(2, chip_sides)
    for j in range(11, LOC):
        down(j)

    red_copies = []
    for k in (2, 1, 3):
        peer = sub_peer(k)
        red_copies.append(
            send(acc.at[pl.ds(LOC, 2), peer[1]], terms.at[u], red_ss.at[k - 1], red_rs.at[k - 1], peer)
        )
    terms[u] = acc[LOC:, u]
    z_step(3)
    merge(0)
    v0 = vr[2 * m]
    v1 = vr[2 * m + 1]
    vm = vq[m, 0]
    merge(-1)
    merge(1)
    for j in range(0, 4):
        prepare_up(j)
    pl.semaphore_wait(relays.at[2], 2)
    z_step(4)
    sep_rhs_copy.wait()
    for copy in red_copies:
        copy.wait_recv()
    prev_copy.wait_recv()
    summed = (terms[0] + terms[1]) + (terms[2] + terms[3])
    delta = jnp.where(s > 0, -times_t(summed[1], prev_inv[...]), 0.0)
    phi = times_t(sep_rhs[u] - summed[0], dinv) + times(delta, vr[i])
    mine[core, 0] = phi
    mine[core, 1] = delta
    mine_copy = send(mine.at[core], mine.at[core], mine_ss, mine_rs, sibling)
    mine_copy.wait_recv()
    phi_chip = mine[1, 0] + times(mine[0, 0], v1)
    part[m, 0] = phi_chip
    part[m, 1] = times_t(mine[0, 0] + mine[1, 1], v0) + mine[0, 1] + times_t(phi_chip, vm)
    ring_copies = []
    for k in far_first:
        ring_copies.append(send(part.at[m], part.at[m], ring_ss.at[k - 1], ring_rs.at[k - 1], chip_peer(k)))

    merge(-2)
    merge(2)
    for j in range(4, 6):
        prepare_up(j)
    z_copies[0, 4, 0].wait_recv()
    z_copies[1, 4, 1].wait_recv()
    f_send(4, 6)
    merge(-3)
    merge(3)
    merge(4)

    eye = (
        lax.broadcasted_iota(jnp.int32, (W, W), 0) == lax.broadcasted_iota(jnp.int32, (W, W), 1)
    ).astype(F32)
    suf_v[CHIPS] = eye
    suf_q[CHIPS] = jnp.zeros((W, W), F32)
    suf_w[CHIPS] = jnp.zeros((ROWS, W), F32)
    pre_v[0] = eye
    pre_z[0] = jnp.zeros((ROWS, W), F32)
    last = CHIPS - 1
    vs, qs = vq[last, 0], vq[last, 1]
    suf_v[last], suf_q[last] = vs, qs
    pv = vq[0, 0]
    pre_v[1] = pv
    for n in reversed(range(last)):
        both = times(vq[n, 0], jnp.concatenate([vs, qs], 1))
        vs = both[:, :W]
        qs = vq[n, 1] + times_t(both[:, W:], vq[n, 0])
        suf_v[n], suf_q[n] = vs, qs
        up = last - n
        if up < last:
            pv = times(pv, vq[up, 0])
            pre_v[up + 1] = pv
    xg[g, 0] = vs
    xg[g, 1] = qs
    x_copies = []
    for k in (2, 1, 3):
        x_copies.append(send(xg.at[g, core], xg.at[g, core], x_ss.at[k - 1], x_rs.at[k - 1], plane_peer(k)))

    for copy in ring_copies:
        copy.wait_recv()

    phis = [part[n, 0] for n in range(CHIPS)]
    xis = [part[n, 1] for n in range(CHIPS)]
    ps, ws, pz = phis[last], xis[last], phis[0]
    suf_w[last] = ws
    pre_z[1] = pz
    for n in reversed(range(last)):
        ps = ps + times(phis[n], suf_v[n + 1])
        ws = xis[n] + times_t(ws + times(phis[n], suf_q[n + 1]), vq[n, 0])
        suf_w[n] = ws
        up = last - n
        if up < last:
            pz = phis[up] + times(pz, vq[up, 0])
            pre_z[up + 1] = pz
    xr[g, 0] = ps
    xr[g, 1] = ws
    r_copies = []
    for k in (2, 1, 3):
        r_copies.append(send(xr.at[g], xr.at[g], r_ss.at[k - 1], r_rs.at[k - 1], plane_peer(k)))
    known_high[...] = jnp.zeros_like(known_high)
    known_low[...] = jnp.zeros_like(known_low)
    h_copies = []
    for k in (1, 3, 2):
        x_copies[(2, 1, 3).index(k)].wait_recv()
        source = lax.rem(g + 4 - k, 4)
        h_copies.append(
            send(xg.at[source, core], xg.at[source, core], h_ss.at[k - 1], h_rs.at[k - 1], sibling)
        )
    for j in range(6, LOC):
        prepare_up(j)
    for copy in h_copies + r_copies:
        copy.wait_recv()

    def group(n):
        return xg[n, 0], xg[n, 1], xr[n, 0], xr[n, 1]

    ga, gb, gc, gd = group(0), group(1), group(2), group(3)
    z1 = ga[2]
    z2 = gb[2] + times(z1, gb[0])
    z3 = gc[2] + times(z2, gc[0])
    w2 = gd[3] + times(z3, gd[1])
    w1 = gc[3] + times(z2, gc[1]) + times_t(w2, gc[0])
    w0 = gb[3] + times(z1, gb[1]) + times_t(w1, gb[0])
    none = jnp.zeros((ROWS, W), F32)
    ends[0, 0], ends[0, 1] = none, w0
    ends[1, 0], ends[1, 1] = z1, w1
    ends[2, 0], ends[2, 1] = z2, w2
    ends[3, 0], ends[3, 1] = z3, none
    z_in = ends[g, 0]
    w_in = ends[g, 1]
    z_chip = pre_z[m] + times(z_in, pre_v[m])
    z_next = part[m, 0] + times(z_chip, vm)
    w_chip = suf_w[m + 1] + times(z_next, suf_q[m + 1]) + times_t(w_in, suf_v[m + 1])
    z_even = mine[0, 0] + times(z_chip, v0)
    odd = mine[1, 0] + times(z_even, v1) + w_chip
    even = z_even + times_t(odd, v1) + mine[1, 1]
    outer = z_chip + times_t(even, v0) + mine[0, 1]
    xs[u, 0] = times(jnp.where(first_core, even, odd), dinv)
    xs[u, 1] = jnp.where(s > 0, times(jnp.where(first_core, outer, even), prev_inv[...]), 0.0)
    fin_copies = []
    for k in (2, 1, 3):
        fin_copies.append(send(xs.at[u], xs.at[u], fin_ss.at[k - 1], fin_rs.at[k - 1], sub_peer(k)))
    for copy in fin_copies:
        copy.wait_recv()

    def learn(t, x):
        high, low = halves(x)
        known_high[t] = high
        known_low[t] = low

    own = jnp.concatenate([xs[v, 0] for v in range(SUBS)], 0)
    own_ref[...] = own
    learn(LOC, own)
    learn(LOC + 1, jnp.concatenate([xs[v, 1] for v in range(SUBS)], 0))
    for j in reversed(range(LOC)):
        places = []
        for k in range(KB):
            target = pat[k, j]
            places.append(jnp.where(target >= 0, target, LOC + 2))
        high = jnp.concatenate([known_high[t] for t in places], 1)
        low = jnp.concatenate([known_low[t] for t in places], 1)
        pulled = folded(jnp.concatenate([high, low], 0), g_high[j], ((1,), (0,)))
        pulled += jnp.dot(high, g_low[j], preferred_element_type=F32)
        x = given[j] - pulled
        learn(j, x)
        x_ref[j] = x

    started = [prev_copy, mine_copy] + list(z_copies.values()) + list(f_copies.values()) + red_copies + ring_copies + r_copies
    for copy in started + x_copies + h_copies + fin_copies:
        copy.wait_send()


def store_kernel(x, own, x_out, own_out, x_sem, own_sem):
    x_copy = pltpu.make_async_copy(x, x_out, x_sem)
    own_copy = pltpu.make_async_copy(own, own_out, own_sem)
    x_copy.start()
    own_copy.start()
    x_copy.wait()
    own_copy.wait()


IN_VMEM = pl.BlockSpec(memory_space=pltpu.VMEM)
IN_SMEM = pl.BlockSpec(memory_space=pltpu.SMEM)
IN_HBM = pl.BlockSpec(memory_space=pltpu.HBM)


def rows_of(*shape):
    return jax.ShapeDtypeStruct(shape, F32)


def shards(rhs_local, diag_inv, off_blocks, pattern, sep_rhs, sep_inv, coupling):
    rhs = rhs_local[0, 0]
    inverse = diag_inv[0, 0]
    blocks = off_blocks[0, 0]
    targets = pattern[0, 0].T
    dma = pltpu.SemaphoreType.DMA
    vmem = pltpu.VMEM
    tree_solution, own = pl.pallas_call(
        solve_kernel,
        name="solve",
        out_shape=(rows_of(LOC, R, W), rows_of(R, W)),
        in_specs=[IN_SMEM] + [IN_HBM] * 6,
        out_specs=(IN_VMEM, IN_VMEM),
        scratch_shapes=[
            vmem((LOC, R, W), F32),
            vmem((SUBS, ROWS, W), F32),
            vmem((W, W), F32),
            vmem((W, W), F32),
            dma((4,)),
            vmem((LOC, W, W), F32),
            vmem((LOC, KB, W, W), F32),
            vmem((LOC + 2, SUBS, ROWS, W), F32),
            vmem((LOC, R, W), F32),
            vmem((W, W), F32),
            vmem((RING, W, W), F32),
            vmem((CHIPS, 2, W, W), F32),
            vmem((CHIPS, 2, ROWS, W), F32),
            vmem((2, 2, ROWS, W), F32),
            vmem((4, 2, W, W), F32),
            vmem((4, 2, ROWS, W), F32),
            vmem((SUBS, 2, ROWS, W), F32),
            vmem((SUBS, 2, ROWS, W), F32),
            vmem((CHIPS + 1, W, W), F32),
            vmem((CHIPS + 1, W, W), F32),
            vmem((CHIPS + 1, ROWS, W), F32),
            vmem((CHIPS, W, W), F32),
            vmem((CHIPS, ROWS, W), F32),
            vmem((4, 2, ROWS, W), F32),
            vmem((LOC, KB * W, W), BF),
            vmem((LOC, KB * W, W), BF),
            vmem((LOC, R, W), F32),
            vmem((LOC + 3, R, W), BF),
            vmem((LOC + 3, R, W), BF),
            dma((5,)), dma((5,)),
            dma(()), dma(()),
            pltpu.SemaphoreType.REGULAR((3,)),
            dma((16,)), dma((16,)),
            dma((8,)), dma((8,)),
            dma((7,)), dma((7,)),
            dma(()), dma(()),
            dma((3,)), dma((3,)),
            dma((3,)), dma((3,)),
            dma((3,)), dma((3,)),
            dma((3,)), dma((3,)),
            dma((3,)), dma((3,)),
        ],
        compiler_params=pltpu.CompilerParams(
            collective_id=0, has_side_effects=True, vmem_limit_bytes=62 << 20
        ),
    )(targets, rhs, inverse, blocks, sep_rhs[0].reshape(SUBS, ROWS, W), sep_inv[0], coupling[0])
    tree_solution, own = pl.pallas_call(
        store_kernel,
        name="store",
        out_shape=(rows_of(LOC, R, W), rows_of(R, W)),
        in_specs=[IN_VMEM, IN_VMEM],
        out_specs=(IN_HBM, IN_HBM),
        scratch_shapes=[dma(()), dma(())],
    )(tree_solution, own)
    return tree_solution[None, None], own[None]


def solution(mesh):
    in_specs = (
        P("seg", "sub", None, None, None),
        P("seg", "sub", None, None, None),
        P("seg", "sub", None, None, None, None),
        P("seg", "sub", None, None),
        P("seg", None, None),
        P("seg", None, None),
        P("seg", None, None),
    )
    out_specs = (P("seg", "sub", None, None, None), P("seg", None, None))
    return jax.shard_map(shards, mesh=mesh, in_specs=in_specs, out_specs=out_specs, check_vma=False)
```

```python
import jax
import jax.numpy as jnp
from jax import lax
from jax.experimental import pallas as pl
from jax.experimental.pallas import tpu as pltpu
from jax.sharding import PartitionSpec as P

BF = jnp.bfloat16
F32 = jnp.float32
MESH = pl.DeviceIdType.MESH
LOC, KB, R, W = 16, 4, 32, 128
SEGS, SUBS = 64, 4
RING, CHIPS, ROWS = 16, 8, 8


def halves(v):
    high = v.astype(BF)
    return high, (v - high.astype(F32)).astype(BF)


def left_operand(v):
    high, low = halves(v)
    top = jnp.concatenate([high, high], 1)
    bottom = jnp.concatenate([low, jnp.zeros_like(low)], 1)
    return jnp.concatenate([top, bottom], 0)


def folded(left, right, dims):
    both = lax.dot_general(left, right, (dims, ((), ())), preferred_element_type=F32)
    half = both.shape[0] // 2
    return both[:half] + both[half:]


def times(v, w):
    high, low = halves(w)
    return folded(left_operand(v), jnp.concatenate([high, low], 0), ((1,), (0,)))


def times_t(v, w):
    high, low = halves(w)
    return folded(left_operand(v), jnp.concatenate([high, low], 1), ((1,), (1,)))


def t_times(w, v):
    return times(w.T, v)


def solve_kernel(
    pat, rhs_hbm, inv_hbm, off_hbm, sep_rhs_hbm, sep_inv_hbm, coupling_hbm,
    x_ref, own_ref,
    rhs, sep_rhs, sep_inv, coupling, small_sem,
    inv, off, acc, ys, prev_inv, vr, vq, part, mine, xg, xr, terms, xs,
    suf_v, suf_q, suf_w, pre_v, pre_z, ends, g_high, g_low, given, known_high, known_low,
    inv_sem, off_sem, prev_ss, prev_rs, relays, z_ss, z_rs, f_ss, f_rs, ring_ss, ring_rs,
    mine_ss, mine_rs, x_ss, x_rs, h_ss, h_rs, r_ss, r_rs, red_ss, red_rs, fin_ss, fin_rs,
):
    s = lax.axis_index("seg")
    u = lax.axis_index("sub")
    core = s % 2
    m = (s // 2) % CHIPS
    i = s % RING
    g = s // RING
    base = s - i
    first_core = core == 0

    def send(src, dst, ss, rs, target):
        copy = pltpu.make_async_remote_copy(
            src_ref=src, dst_ref=dst, send_sem=ss, recv_sem=rs, device_id=target, device_id_type=MESH
        )
        copy.start()
        return copy

    def local(hbm, vmem, sem):
        copy = pltpu.make_async_copy(hbm, vmem, sem)
        copy.start()
        return copy

    sibling = (s + 1 - 2 * core, u)
    after = (lax.rem(s + 1, SEGS), u)
    before = (lax.rem(s + SEGS - 1, SEGS), u)

    def chip_peer(k):
        return (base + lax.rem(i + 2 * k, RING), u)

    def plane_peer(k):
        return (lax.rem(s + RING * k, SEGS), u)

    def sub_peer(k):
        return (s, lax.rem(u + k, SUBS))

    barrier = pltpu.get_barrier_semaphore()
    far_first = (4, 3, 5, 2, 6, 1, 7)
    chip_sides = (chip_peer(1), chip_peer(CHIPS - 1))
    greeted = [after, before, sibling, *chip_sides]
    greeted += [plane_peer(1), plane_peer(3), sub_peer(1), sub_peer(3)]
    for peer in greeted:
        pl.semaphore_signal(barrier, inc=1, device_id=peer, device_id_type=MESH)

    rhs_copy = local(rhs_hbm, rhs, small_sem.at[2])
    tree_copies = {}
    for n, (low, high) in enumerate(((0, 1), (1, 2), (2, 4), (4, 8), (8, 16))):
        run = pl.ds(low, high - low)
        tree_copies[low] = (
            local(inv_hbm.at[run], inv.at[run], inv_sem.at[n]),
            local(off_hbm.at[run], off.at[run], off_sem.at[n]),
        )
        if n == 1:
            sep_inv_copy = local(sep_inv_hbm, sep_inv, small_sem.at[0])
            coupling_copy = local(coupling_hbm, coupling, small_sem.at[1])
    sep_rhs_copy = local(sep_rhs_hbm, sep_rhs, small_sem.at[3])

    acc[...] = jnp.zeros_like(acc)
    rhs_copy.wait()

    def down(j):
        for copy in tree_copies.get(j, ()):
            copy.wait()
        y = times_t(rhs[j] - acc[j].reshape(R, W), inv[j])
        ys[j] = y
        products = times_t(y, off[j].reshape(KB * W, W))
        width = LOC + 1 - j
        ids = lax.broadcasted_iota(jnp.int32, (width, 1, ROWS, W), 0) + (j + 1)
        total = acc[j + 1 :]
        for k in range(KB):
            piece = products[:, k * W : (k + 1) * W].reshape(1, SUBS, ROWS, W)
            total = total + jnp.where(ids == pat[k, j], piece, 0.0)
        acc[j + 1 :] = total

    def prepare_up(j):
        stacked = jnp.concatenate([off[j].reshape(KB * W, W), ys[j]], 0)
        both = times(stacked, inv[j])
        high, low = halves(both[: KB * W])
        g_high[j] = high
        g_low[j] = low
        given[j] = both[KB * W :]

    z_copies = {}
    f_copies = {}

    def chip_at(distance):
        return lax.rem(m + CHIPS + distance, CHIPS)

    def z_send(way, step, piece):
        source = 2 * chip_at(1 - step if way == 0 else step - 1) + core
        where = vr.at[source, pl.ds(piece * (W // 2), W // 2)]
        index = way * 8 + (step - 1) * 2 + piece
        z_copies[way, step, piece] = send(where, where, z_ss.at[index], z_rs.at[index], chip_sides[way])

    def f_send(distance, index):
        where = vr.at[2 * chip_at(distance) + core]
        f_copies[distance] = send(where, where, f_ss.at[index], f_rs.at[index], sibling)

    def z_step(step):
        for piece in range(2):
            for way in range(2):
                z_copies[way, step - 1, piece].wait_recv()
                if step < 4 or way == piece:
                    z_send(way, step, piece)
        f_send(1 - step, step - 2)
        f_send(step - 1, step + 1)

    def merge(distance):
        f_copies[distance].wait_recv()
        chip = chip_at(distance)
        first, second = vr[2 * chip], vr[2 * chip + 1]
        pair = times(first, second)
        vq[chip, 0] = pair
        vq[chip, 1] = times_t(first, first) + times_t(pair, pair)

    def relay(level, peers):
        for peer in peers:
            pl.semaphore_signal(relays.at[level], inc=1, device_id=peer, device_id_type=MESH)

    down(0)
    sep_inv_copy.wait()
    coupling_copy.wait()
    dinv = sep_inv[...]
    own_v = -times(dinv, coupling[...]).T
    own_v = jnp.where(s > 0, own_v, 0.0)
    vr[i] = own_v
    down(1)

    pl.semaphore_wait(barrier, len(greeted))
    for piece in range(2):
        for way in range(2):
            z_send(way, 1, piece)
    f_send(0, 7)
    prev_copy = send(sep_inv, prev_inv, prev_ss, prev_rs, after)
    relay(0, [*chip_sides, plane_peer(3), sub_peer(3)])
    for j in range(2, 6):
        down(j)
    pl.semaphore_wait(relays.at[0], 4)
    relay(1, chip_sides)
    for j in range(6, 9):
        down(j)
    z_step(2)
    for j in range(9, 11):
        down(j)
    pl.semaphore_wait(relays.at[1], 2)
    relay(2, chip_sides)
    for j in range(11, LOC):
        down(j)

    red_copies = []
    for k in (2, 1, 3):
        peer = sub_peer(k)
        red_copies.append(
            send(acc.at[pl.ds(LOC, 2), peer[1]], terms.at[u], red_ss.at[k - 1], red_rs.at[k - 1], peer)
        )
    terms[u] = acc[LOC:, u]
    z_step(3)
    merge(0)
    v0 = vr[2 * m]
    v1 = vr[2 * m + 1]
    vm = vq[m, 0]
    merge(-1)
    merge(1)
    for j in range(0, 4):
        prepare_up(j)
    pl.semaphore_wait(relays.at[2], 2)
    z_step(4)
    sep_rhs_copy.wait()
    for copy in red_copies:
        copy.wait_recv()
    prev_copy.wait_recv()
    summed = (terms[0] + terms[1]) + (terms[2] + terms[3])
    delta = jnp.where(s > 0, -times_t(summed[1], prev_inv[...]), 0.0)
    phi = times_t(sep_rhs[u] - summed[0], dinv) + times(delta, vr[i])
    mine[core, 0] = phi
    mine[core, 1] = delta
    mine_copy = send(mine.at[core], mine.at[core], mine_ss, mine_rs, sibling)
    mine_copy.wait_recv()
    phi_chip = mine[1, 0] + times(mine[0, 0], v1)
    part[m, 0] = phi_chip
    part[m, 1] = times_t(mine[0, 0] + mine[1, 1], v0) + mine[0, 1] + times_t(phi_chip, vm)
    ring_copies = []
    for k in far_first:
        ring_copies.append(send(part.at[m], part.at[m], ring_ss.at[k - 1], ring_rs.at[k - 1], chip_peer(k)))

    merge(-2)
    merge(2)
    for j in range(4, 6):
        prepare_up(j)
    z_copies[0, 4, 0].wait_recv()
    z_copies[1, 4, 1].wait_recv()
    f_send(4, 6)
    merge(-3)
    merge(3)
    merge(4)

    eye = (
        lax.broadcasted_iota(jnp.int32, (W, W), 0) == lax.broadcasted_iota(jnp.int32, (W, W), 1)
    ).astype(F32)
    suf_v[CHIPS] = eye
    suf_q[CHIPS] = jnp.zeros((W, W), F32)
    suf_w[CHIPS] = jnp.zeros((ROWS, W), F32)
    pre_v[0] = eye
    pre_z[0] = jnp.zeros((ROWS, W), F32)
    level = [(vq[n, 0], vq[n, 1]) for n in range(CHIPS)]
    while len(level) > 1:
        merged = []
        for (va, qa), (vb, qb) in zip(level[::2], level[1::2]):
            both = times(va, jnp.concatenate([vb, qb], 1))
            merged.append((both[:, :W], qa + times_t(both[:, W:], va)))
        level = merged
    vs, qs = level[0]
    xg[g, 0] = vs
    xg[g, 1] = qs
    x_copies = []
    for k in (2, 1, 3):
        x_copies.append(send(xg.at[g, core], xg.at[g, core], x_ss.at[k - 1], x_rs.at[k - 1], plane_peer(k)))

    last = CHIPS - 1
    vs, qs = vq[last, 0], vq[last, 1]
    suf_v[last], suf_q[last] = vs, qs
    pv = vq[0, 0]
    pre_v[1] = pv
    for n in reversed(range(1, last)):
        both = times(vq[n, 0], jnp.concatenate([vs, qs], 1))
        vs = both[:, :W]
        qs = vq[n, 1] + times_t(both[:, W:], vq[n, 0])
        suf_v[n], suf_q[n] = vs, qs
        up = last - n
        if up < last:
            pv = times(pv, vq[up, 0])
            pre_v[up + 1] = pv
    for copy in ring_copies:
        copy.wait_recv()

    phis = [part[n, 0] for n in range(CHIPS)]
    xis = [part[n, 1] for n in range(CHIPS)]
    ps, ws, pz = phis[last], xis[last], phis[0]
    suf_w[last] = ws
    pre_z[1] = pz
    for n in reversed(range(last)):
        ps = ps + times(phis[n], suf_v[n + 1])
        ws = xis[n] + times_t(ws + times(phis[n], suf_q[n + 1]), vq[n, 0])
        suf_w[n] = ws
        up = last - n
        if up < last:
            pz = phis[up] + times(pz, vq[up, 0])
            pre_z[up + 1] = pz
    xr[g, 0] = ps
    xr[g, 1] = ws
    r_copies = []
    for k in (2, 1, 3):
        r_copies.append(send(xr.at[g], xr.at[g], r_ss.at[k - 1], r_rs.at[k - 1], plane_peer(k)))
    known_high[...] = jnp.zeros_like(known_high)
    known_low[...] = jnp.zeros_like(known_low)
    h_copies = []
    for k in (1, 3, 2):
        x_copies[(2, 1, 3).index(k)].wait_recv()
        source = lax.rem(g + 4 - k, 4)
        h_copies.append(
            send(xg.at[source, core], xg.at[source, core], h_ss.at[k - 1], h_rs.at[k - 1], sibling)
        )
    for j in range(6, LOC):
        prepare_up(j)
    for copy in h_copies + r_copies:
        copy.wait_recv()

    def group(n):
        return xg[n, 0], xg[n, 1], xr[n, 0], xr[n, 1]

    ga, gb, gc, gd = group(0), group(1), group(2), group(3)
    z1 = ga[2]
    z2 = gb[2] + times(z1, gb[0])
    z3 = gc[2] + times(z2, gc[0])
    w2 = gd[3] + times(z3, gd[1])
    w1 = gc[3] + times(z2, gc[1]) + times_t(w2, gc[0])
    w0 = gb[3] + times(z1, gb[1]) + times_t(w1, gb[0])
    none = jnp.zeros((ROWS, W), F32)
    ends[0, 0], ends[0, 1] = none, w0
    ends[1, 0], ends[1, 1] = z1, w1
    ends[2, 0], ends[2, 1] = z2, w2
    ends[3, 0], ends[3, 1] = z3, none
    z_in = ends[g, 0]
    w_in = ends[g, 1]
    z_chip = pre_z[m] + times(z_in, pre_v[m])
    z_next = part[m, 0] + times(z_chip, vm)
    w_chip = suf_w[m + 1] + times(z_next, suf_q[m + 1]) + times_t(w_in, suf_v[m + 1])
    z_even = mine[0, 0] + times(z_chip, v0)
    odd = mine[1, 0] + times(z_even, v1) + w_chip
    even = z_even + times_t(odd, v1) + mine[1, 1]
    outer = z_chip + times_t(even, v0) + mine[0, 1]
    xs[u, 0] = times(jnp.where(first_core, even, odd), dinv)
    xs[u, 1] = jnp.where(s > 0, times(jnp.where(first_core, outer, even), prev_inv[...]), 0.0)
    fin_copies = []
    for k in (2, 1, 3):
        fin_copies.append(send(xs.at[u], xs.at[u], fin_ss.at[k - 1], fin_rs.at[k - 1], sub_peer(k)))
    for copy in fin_copies:
        copy.wait_recv()

    def learn(t, x):
        high, low = halves(x)
        known_high[t] = high
        known_low[t] = low

    own = jnp.concatenate([xs[v, 0] for v in range(SUBS)], 0)
    own_ref[...] = own
    learn(LOC, own)
    learn(LOC + 1, jnp.concatenate([xs[v, 1] for v in range(SUBS)], 0))
    for j in reversed(range(LOC)):
        places = []
        for k in range(KB):
            target = pat[k, j]
            places.append(jnp.where(target >= 0, target, LOC + 2))
        high = jnp.concatenate([known_high[t] for t in places], 1)
        low = jnp.concatenate([known_low[t] for t in places], 1)
        pulled = folded(jnp.concatenate([high, low], 0), g_high[j], ((1,), (0,)))
        pulled += jnp.dot(high, g_low[j], preferred_element_type=F32)
        x = given[j] - pulled
        learn(j, x)
        x_ref[j] = x

    started = [prev_copy, mine_copy] + list(z_copies.values()) + list(f_copies.values()) + red_copies + ring_copies + r_copies
    for copy in started + x_copies + h_copies + fin_copies:
        copy.wait_send()


def store_kernel(x, own, x_out, own_out, x_sem, own_sem):
    x_copy = pltpu.make_async_copy(x, x_out, x_sem)
    own_copy = pltpu.make_async_copy(own, own_out, own_sem)
    x_copy.start()
    own_copy.start()
    x_copy.wait()
    own_copy.wait()


IN_VMEM = pl.BlockSpec(memory_space=pltpu.VMEM)
IN_SMEM = pl.BlockSpec(memory_space=pltpu.SMEM)
IN_HBM = pl.BlockSpec(memory_space=pltpu.HBM)


def rows_of(*shape):
    return jax.ShapeDtypeStruct(shape, F32)


def shards(rhs_local, diag_inv, off_blocks, pattern, sep_rhs, sep_inv, coupling):
    rhs = rhs_local[0, 0]
    inverse = diag_inv[0, 0]
    blocks = off_blocks[0, 0]
    targets = pattern[0, 0].T
    dma = pltpu.SemaphoreType.DMA
    vmem = pltpu.VMEM
    tree_solution, own = pl.pallas_call(
        solve_kernel,
        name="solve",
        out_shape=(rows_of(LOC, R, W), rows_of(R, W)),
        in_specs=[IN_SMEM] + [IN_HBM] * 6,
        out_specs=(IN_VMEM, IN_VMEM),
        scratch_shapes=[
            vmem((LOC, R, W), F32),
            vmem((SUBS, ROWS, W), F32),
            vmem((W, W), F32),
            vmem((W, W), F32),
            dma((4,)),
            vmem((LOC, W, W), F32),
            vmem((LOC, KB, W, W), F32),
            vmem((LOC + 2, SUBS, ROWS, W), F32),
            vmem((LOC, R, W), F32),
            vmem((W, W), F32),
            vmem((RING, W, W), F32),
            vmem((CHIPS, 2, W, W), F32),
            vmem((CHIPS, 2, ROWS, W), F32),
            vmem((2, 2, ROWS, W), F32),
            vmem((4, 2, W, W), F32),
            vmem((4, 2, ROWS, W), F32),
            vmem((SUBS, 2, ROWS, W), F32),
            vmem((SUBS, 2, ROWS, W), F32),
            vmem((CHIPS + 1, W, W), F32),
            vmem((CHIPS + 1, W, W), F32),
            vmem((CHIPS + 1, ROWS, W), F32),
            vmem((CHIPS, W, W), F32),
            vmem((CHIPS, ROWS, W), F32),
            vmem((4, 2, ROWS, W), F32),
            vmem((LOC, KB * W, W), BF),
            vmem((LOC, KB * W, W), BF),
            vmem((LOC, R, W), F32),
            vmem((LOC + 3, R, W), BF),
            vmem((LOC + 3, R, W), BF),
            dma((5,)), dma((5,)),
            dma(()), dma(()),
            pltpu.SemaphoreType.REGULAR((3,)),
            dma((16,)), dma((16,)),
            dma((8,)), dma((8,)),
            dma((7,)), dma((7,)),
            dma(()), dma(()),
            dma((3,)), dma((3,)),
            dma((3,)), dma((3,)),
            dma((3,)), dma((3,)),
            dma((3,)), dma((3,)),
            dma((3,)), dma((3,)),
        ],
        compiler_params=pltpu.CompilerParams(
            collective_id=0, has_side_effects=True, vmem_limit_bytes=62 << 20
        ),
    )(targets, rhs, inverse, blocks, sep_rhs[0].reshape(SUBS, ROWS, W), sep_inv[0], coupling[0])
    tree_solution, own = pl.pallas_call(
        store_kernel,
        name="store",
        out_shape=(rows_of(LOC, R, W), rows_of(R, W)),
        in_specs=[IN_VMEM, IN_VMEM],
        out_specs=(IN_HBM, IN_HBM),
        scratch_shapes=[dma(()), dma(())],
    )(tree_solution, own)
    return tree_solution[None, None], own[None]


def solution(mesh):
    in_specs = (
        P("seg", "sub", None, None, None),
        P("seg", "sub", None, None, None),
        P("seg", "sub", None, None, None, None),
        P("seg", "sub", None, None),
        P("seg", None, None),
        P("seg", None, None),
        P("seg", None, None),
    )
    out_specs = (P("seg", "sub", None, None, None), P("seg", None, None))
    return jax.shard_map(shards, mesh=mesh, in_specs=in_specs, out_specs=out_specs, check_vma=False)
```

```python
import jax
import jax.numpy as jnp
from jax import lax
from jax.experimental import pallas as pl
from jax.experimental.pallas import tpu as pltpu
from jax.sharding import PartitionSpec as P

BF = jnp.bfloat16
F32 = jnp.float32
MESH = pl.DeviceIdType.MESH
LOC, KB, R, W = 16, 4, 32, 128
SEGS, SUBS = 64, 4
RING, CHIPS, ROWS = 16, 8, 8


def halves(v):
    high = v.astype(BF)
    return high, (v - high.astype(F32)).astype(BF)


def left_operand(v):
    high, low = halves(v)
    top = jnp.concatenate([high, high], 1)
    bottom = jnp.concatenate([low, jnp.zeros_like(low)], 1)
    return jnp.concatenate([top, bottom], 0)


def folded(left, right, dims):
    both = lax.dot_general(left, right, (dims, ((), ())), preferred_element_type=F32)
    half = both.shape[0] // 2
    return both[:half] + both[half:]


def times(v, w):
    high, low = halves(w)
    return folded(left_operand(v), jnp.concatenate([high, low], 0), ((1,), (0,)))


def times_t(v, w):
    high, low = halves(w)
    return folded(left_operand(v), jnp.concatenate([high, low], 1), ((1,), (1,)))


def t_times(w, v):
    return times(w.T, v)


def solve_kernel(
    pat, rhs_hbm, inv_hbm, off_hbm, sep_rhs_hbm, sep_inv_hbm, coupling_hbm,
    x_ref, own_ref,
    rhs, sep_rhs, sep_inv, coupling, small_sem,
    inv, off, acc, ys, prev_inv, vr, vq, part, mine, xg, xr, terms, xs,
    suf_v, suf_q, suf_w, pre_v, pre_z, ends, g_high, g_low, given, known_high, known_low,
    inv_sem, off_sem, prev_ss, prev_rs, relays, z_ss, z_rs, f_ss, f_rs, ring_ss, ring_rs,
    mine_ss, mine_rs, x_ss, x_rs, h_ss, h_rs, r_ss, r_rs, red_ss, red_rs, fin_ss, fin_rs,
):
    s = lax.axis_index("seg")
    u = lax.axis_index("sub")
    core = s % 2
    m = (s // 2) % CHIPS
    i = s % RING
    g = s // RING
    base = s - i
    first_core = core == 0

    def send(src, dst, ss, rs, target):
        copy = pltpu.make_async_remote_copy(
            src_ref=src, dst_ref=dst, send_sem=ss, recv_sem=rs, device_id=target, device_id_type=MESH
        )
        copy.start()
        return copy

    def local(hbm, vmem, sem):
        copy = pltpu.make_async_copy(hbm, vmem, sem)
        copy.start()
        return copy

    sibling = (s + 1 - 2 * core, u)
    after = (lax.rem(s + 1, SEGS), u)
    before = (lax.rem(s + SEGS - 1, SEGS), u)

    def chip_peer(k):
        return (base + lax.rem(i + 2 * k, RING), u)

    def plane_peer(k):
        return (lax.rem(s + RING * k, SEGS), u)

    def sub_peer(k):
        return (s, lax.rem(u + k, SUBS))

    barrier = pltpu.get_barrier_semaphore()
    far_first = (4, 3, 5, 2, 6, 1, 7)
    chip_sides = (chip_peer(1), chip_peer(CHIPS - 1))
    greeted = [after, before, sibling, *chip_sides]
    greeted += [plane_peer(1), plane_peer(3), sub_peer(1), sub_peer(3)]
    for peer in greeted:
        pl.semaphore_signal(barrier, inc=1, device_id=peer, device_id_type=MESH)

    rhs_copy = local(rhs_hbm, rhs, small_sem.at[2])
    tree_copies = {}
    for n, (low, high) in enumerate(((0, 1), (1, 2), (2, 4), (4, 8), (8, 16))):
        run = pl.ds(low, high - low)
        tree_copies[low] = (
            local(inv_hbm.at[run], inv.at[run], inv_sem.at[n]),
            local(off_hbm.at[run], off.at[run], off_sem.at[n]),
        )
        if n == 1:
            sep_inv_copy = local(sep_inv_hbm, sep_inv, small_sem.at[0])
            coupling_copy = local(coupling_hbm, coupling, small_sem.at[1])
    sep_rhs_copy = local(sep_rhs_hbm, sep_rhs, small_sem.at[3])

    acc[...] = jnp.zeros_like(acc)
    rhs_copy.wait()

    def down(j):
        for copy in tree_copies.get(j, ()):
            copy.wait()
        y = times_t(rhs[j] - acc[j].reshape(R, W), inv[j])
        ys[j] = y
        products = times_t(y, off[j].reshape(KB * W, W))
        width = LOC + 1 - j
        ids = lax.broadcasted_iota(jnp.int32, (width, 1, ROWS, W), 0) + (j + 1)
        total = acc[j + 1 :]
        for k in range(KB):
            piece = products[:, k * W : (k + 1) * W].reshape(1, SUBS, ROWS, W)
            total = total + jnp.where(ids == pat[k, j], piece, 0.0)
        acc[j + 1 :] = total

    def prepare_up(j):
        stacked = jnp.concatenate([off[j].reshape(KB * W, W), ys[j]], 0)
        both = times(stacked, inv[j])
        high, low = halves(both[: KB * W])
        g_high[j] = high
        g_low[j] = low
        given[j] = both[KB * W :]

    z_copies = {}
    f_copies = {}

    def chip_at(distance):
        return lax.rem(m + CHIPS + distance, CHIPS)

    def z_send(way, step, piece):
        source = 2 * chip_at(1 - step if way == 0 else step - 1) + core
        where = vr.at[source, pl.ds(piece * (W // 2), W // 2)]
        index = way * 8 + (step - 1) * 2 + piece
        z_copies[way, step, piece] = send(where, where, z_ss.at[index], z_rs.at[index], chip_sides[way])

    def f_send(distance, index):
        where = vr.at[2 * chip_at(distance) + core]
        f_copies[distance] = send(where, where, f_ss.at[index], f_rs.at[index], sibling)

    def z_step(step):
        for piece in range(2):
            for way in range(2):
                z_copies[way, step - 1, piece].wait_recv()
                if step < 4 or way == piece:
                    z_send(way, step, piece)
        f_send(1 - step, step - 2)
        f_send(step - 1, step + 1)

    def merge(distance):
        f_copies[distance].wait_recv()
        chip = chip_at(distance)
        first, second = vr[2 * chip], vr[2 * chip + 1]
        pair = times(first, second)
        vq[chip, 0] = pair
        vq[chip, 1] = times_t(first, first) + times_t(pair, pair)

    def relay(level, peers):
        for peer in peers:
            pl.semaphore_signal(relays.at[level], inc=1, device_id=peer, device_id_type=MESH)

    down(0)
    sep_inv_copy.wait()
    coupling_copy.wait()
    dinv = sep_inv[...]
    own_v = -times(dinv, coupling[...]).T
    own_v = jnp.where(s > 0, own_v, 0.0)
    vr[i] = own_v
    down(1)

    pl.semaphore_wait(barrier, len(greeted))
    for piece in range(2):
        for way in range(2):
            z_send(way, 1, piece)
    f_send(0, 7)
    relay(0, [*chip_sides, plane_peer(3), sub_peer(3)])
    for j in range(2, 6):
        down(j)
    pl.semaphore_wait(relays.at[0], 4)
    relay(1, chip_sides)
    for j in range(6, 9):
        down(j)
    z_step(2)
    prev_copy = send(sep_inv, prev_inv, prev_ss, prev_rs, after)
    for j in range(9, 11):
        down(j)
    pl.semaphore_wait(relays.at[1], 2)
    relay(2, chip_sides)
    for j in range(11, LOC):
        down(j)

    red_copies = []
    for k in (2, 1, 3):
        peer = sub_peer(k)
        red_copies.append(
            send(acc.at[pl.ds(LOC, 2), peer[1]], terms.at[u], red_ss.at[k - 1], red_rs.at[k - 1], peer)
        )
    terms[u] = acc[LOC:, u]
    z_step(3)
    merge(0)
    v0 = vr[2 * m]
    v1 = vr[2 * m + 1]
    vm = vq[m, 0]
    merge(-1)
    merge(1)
    for j in range(0, 4):
        prepare_up(j)
    pl.semaphore_wait(relays.at[2], 2)
    z_step(4)
    sep_rhs_copy.wait()
    for copy in red_copies:
        copy.wait_recv()
    prev_copy.wait_recv()
    summed = (terms[0] + terms[1]) + (terms[2] + terms[3])
    delta = jnp.where(s > 0, -times_t(summed[1], prev_inv[...]), 0.0)
    phi = times_t(sep_rhs[u] - summed[0], dinv) + times(delta, vr[i])
    mine[core, 0] = phi
    mine[core, 1] = delta
    mine_copy = send(mine.at[core], mine.at[core], mine_ss, mine_rs, sibling)
    mine_copy.wait_recv()
    phi_chip = mine[1, 0] + times(mine[0, 0], v1)
    part[m, 0] = phi_chip
    part[m, 1] = times_t(mine[0, 0] + mine[1, 1], v0) + mine[0, 1] + times_t(phi_chip, vm)
    ring_copies = []
    for k in far_first:
        ring_copies.append(send(part.at[m], part.at[m], ring_ss.at[k - 1], ring_rs.at[k - 1], chip_peer(k)))

    merge(-2)
    merge(2)
    for j in range(4, 6):
        prepare_up(j)
    z_copies[0, 4, 0].wait_recv()
    z_copies[1, 4, 1].wait_recv()
    f_send(4, 6)
    merge(-3)
    merge(3)
    merge(4)

    eye = (
        lax.broadcasted_iota(jnp.int32, (W, W), 0) == lax.broadcasted_iota(jnp.int32, (W, W), 1)
    ).astype(F32)
    suf_v[CHIPS] = eye
    suf_q[CHIPS] = jnp.zeros((W, W), F32)
    suf_w[CHIPS] = jnp.zeros((ROWS, W), F32)
    pre_v[0] = eye
    pre_z[0] = jnp.zeros((ROWS, W), F32)
    level = [(vq[n, 0], vq[n, 1]) for n in range(CHIPS)]
    while len(level) > 1:
        merged = []
        for (va, qa), (vb, qb) in zip(level[::2], level[1::2]):
            both = times(va, jnp.concatenate([vb, qb], 1))
            merged.append((both[:, :W], qa + times_t(both[:, W:], va)))
        level = merged
    vs, qs = level[0]
    xg[g, 0] = vs
    xg[g, 1] = qs
    x_copies = []
    for k in (2, 1, 3):
        x_copies.append(send(xg.at[g, core], xg.at[g, core], x_ss.at[k - 1], x_rs.at[k - 1], plane_peer(k)))

    last = CHIPS - 1
    vs, qs = vq[last, 0], vq[last, 1]
    suf_v[last], suf_q[last] = vs, qs
    pv = vq[0, 0]
    pre_v[1] = pv
    for n in reversed(range(1, last)):
        both = times(vq[n, 0], jnp.concatenate([vs, qs], 1))
        vs = both[:, :W]
        qs = vq[n, 1] + times_t(both[:, W:], vq[n, 0])
        suf_v[n], suf_q[n] = vs, qs
        up = last - n
        if up < last:
            pv = times(pv, vq[up, 0])
            pre_v[up + 1] = pv
    for copy in ring_copies:
        copy.wait_recv()

    phis = [part[n, 0] for n in range(CHIPS)]
    xis = [part[n, 1] for n in range(CHIPS)]
    ps, ws, pz = phis[last], xis[last], phis[0]
    suf_w[last] = ws
    pre_z[1] = pz
    for n in reversed(range(last)):
        ps = ps + times(phis[n], suf_v[n + 1])
        ws = xis[n] + times_t(ws + times(phis[n], suf_q[n + 1]), vq[n, 0])
        suf_w[n] = ws
        up = last - n
        if up < last:
            pz = phis[up] + times(pz, vq[up, 0])
            pre_z[up + 1] = pz
    xr[g, 0] = ps
    xr[g, 1] = ws
    r_copies = []
    for k in (2, 1, 3):
        r_copies.append(send(xr.at[g], xr.at[g], r_ss.at[k - 1], r_rs.at[k - 1], plane_peer(k)))
    known_high[...] = jnp.zeros_like(known_high)
    known_low[...] = jnp.zeros_like(known_low)
    h_copies = []
    for k in (1, 3, 2):
        x_copies[(2, 1, 3).index(k)].wait_recv()
        source = lax.rem(g + 4 - k, 4)
        h_copies.append(
            send(xg.at[source, core], xg.at[source, core], h_ss.at[k - 1], h_rs.at[k - 1], sibling)
        )
    for j in range(6, LOC):
        prepare_up(j)
    for copy in h_copies + r_copies:
        copy.wait_recv()

    def group(n):
        return xg[n, 0], xg[n, 1], xr[n, 0], xr[n, 1]

    ga, gb, gc, gd = group(0), group(1), group(2), group(3)
    z1 = ga[2]
    z2 = gb[2] + times(z1, gb[0])
    z3 = gc[2] + times(z2, gc[0])
    w2 = gd[3] + times(z3, gd[1])
    w1 = gc[3] + times(z2, gc[1]) + times_t(w2, gc[0])
    w0 = gb[3] + times(z1, gb[1]) + times_t(w1, gb[0])
    none = jnp.zeros((ROWS, W), F32)
    ends[0, 0], ends[0, 1] = none, w0
    ends[1, 0], ends[1, 1] = z1, w1
    ends[2, 0], ends[2, 1] = z2, w2
    ends[3, 0], ends[3, 1] = z3, none
    z_in = ends[g, 0]
    w_in = ends[g, 1]
    z_chip = pre_z[m] + times(z_in, pre_v[m])
    z_next = part[m, 0] + times(z_chip, vm)
    w_chip = suf_w[m + 1] + times(z_next, suf_q[m + 1]) + times_t(w_in, suf_v[m + 1])
    z_even = mine[0, 0] + times(z_chip, v0)
    odd = mine[1, 0] + times(z_even, v1) + w_chip
    even = z_even + times_t(odd, v1) + mine[1, 1]
    outer = z_chip + times_t(even, v0) + mine[0, 1]
    xs[u, 0] = times(jnp.where(first_core, even, odd), dinv)
    xs[u, 1] = jnp.where(s > 0, times(jnp.where(first_core, outer, even), prev_inv[...]), 0.0)
    fin_copies = []
    for k in (2, 1, 3):
        fin_copies.append(send(xs.at[u], xs.at[u], fin_ss.at[k - 1], fin_rs.at[k - 1], sub_peer(k)))
    for copy in fin_copies:
        copy.wait_recv()

    def learn(t, x):
        high, low = halves(x)
        known_high[t] = high
        known_low[t] = low

    own = jnp.concatenate([xs[v, 0] for v in range(SUBS)], 0)
    own_ref[...] = own
    learn(LOC, own)
    learn(LOC + 1, jnp.concatenate([xs[v, 1] for v in range(SUBS)], 0))
    for j in reversed(range(LOC)):
        places = []
        for k in range(KB):
            target = pat[k, j]
            places.append(jnp.where(target >= 0, target, LOC + 2))
        high = jnp.concatenate([known_high[t] for t in places], 1)
        low = jnp.concatenate([known_low[t] for t in places], 1)
        pulled = folded(jnp.concatenate([high, low], 0), g_high[j], ((1,), (0,)))
        pulled += jnp.dot(high, g_low[j], preferred_element_type=F32)
        x = given[j] - pulled
        learn(j, x)
        x_ref[j] = x

    started = [prev_copy, mine_copy] + list(z_copies.values()) + list(f_copies.values()) + red_copies + ring_copies + r_copies
    for copy in started + x_copies + h_copies + fin_copies:
        copy.wait_send()


def store_kernel(x, own, x_out, own_out, x_sem, own_sem):
    x_copy = pltpu.make_async_copy(x, x_out, x_sem)
    own_copy = pltpu.make_async_copy(own, own_out, own_sem)
    x_copy.start()
    own_copy.start()
    x_copy.wait()
    own_copy.wait()


IN_VMEM = pl.BlockSpec(memory_space=pltpu.VMEM)
IN_SMEM = pl.BlockSpec(memory_space=pltpu.SMEM)
IN_HBM = pl.BlockSpec(memory_space=pltpu.HBM)


def rows_of(*shape):
    return jax.ShapeDtypeStruct(shape, F32)


def shards(rhs_local, diag_inv, off_blocks, pattern, sep_rhs, sep_inv, coupling):
    rhs = rhs_local[0, 0]
    inverse = diag_inv[0, 0]
    blocks = off_blocks[0, 0]
    targets = pattern[0, 0].T
    dma = pltpu.SemaphoreType.DMA
    vmem = pltpu.VMEM
    tree_solution, own = pl.pallas_call(
        solve_kernel,
        name="solve",
        out_shape=(rows_of(LOC, R, W), rows_of(R, W)),
        in_specs=[IN_SMEM] + [IN_HBM] * 6,
        out_specs=(IN_VMEM, IN_VMEM),
        scratch_shapes=[
            vmem((LOC, R, W), F32),
            vmem((SUBS, ROWS, W), F32),
            vmem((W, W), F32),
            vmem((W, W), F32),
            dma((4,)),
            vmem((LOC, W, W), F32),
            vmem((LOC, KB, W, W), F32),
            vmem((LOC + 2, SUBS, ROWS, W), F32),
            vmem((LOC, R, W), F32),
            vmem((W, W), F32),
            vmem((RING, W, W), F32),
            vmem((CHIPS, 2, W, W), F32),
            vmem((CHIPS, 2, ROWS, W), F32),
            vmem((2, 2, ROWS, W), F32),
            vmem((4, 2, W, W), F32),
            vmem((4, 2, ROWS, W), F32),
            vmem((SUBS, 2, ROWS, W), F32),
            vmem((SUBS, 2, ROWS, W), F32),
            vmem((CHIPS + 1, W, W), F32),
            vmem((CHIPS + 1, W, W), F32),
            vmem((CHIPS + 1, ROWS, W), F32),
            vmem((CHIPS, W, W), F32),
            vmem((CHIPS, ROWS, W), F32),
            vmem((4, 2, ROWS, W), F32),
            vmem((LOC, KB * W, W), BF),
            vmem((LOC, KB * W, W), BF),
            vmem((LOC, R, W), F32),
            vmem((LOC + 3, R, W), BF),
            vmem((LOC + 3, R, W), BF),
            dma((5,)), dma((5,)),
            dma(()), dma(()),
            pltpu.SemaphoreType.REGULAR((3,)),
            dma((16,)), dma((16,)),
            dma((8,)), dma((8,)),
            dma((7,)), dma((7,)),
            dma(()), dma(()),
            dma((3,)), dma((3,)),
            dma((3,)), dma((3,)),
            dma((3,)), dma((3,)),
            dma((3,)), dma((3,)),
            dma((3,)), dma((3,)),
        ],
        compiler_params=pltpu.CompilerParams(
            collective_id=0, has_side_effects=True, vmem_limit_bytes=62 << 20
        ),
    )(targets, rhs, inverse, blocks, sep_rhs[0].reshape(SUBS, ROWS, W), sep_inv[0], coupling[0])
    tree_solution, own = pl.pallas_call(
        store_kernel,
        name="store",
        out_shape=(rows_of(LOC, R, W), rows_of(R, W)),
        in_specs=[IN_VMEM, IN_VMEM],
        out_specs=(IN_HBM, IN_HBM),
        scratch_shapes=[dma(()), dma(())],
    )(tree_solution, own)
    return tree_solution[None, None], own[None]


def solution(mesh):
    in_specs = (
        P("seg", "sub", None, None, None),
        P("seg", "sub", None, None, None),
        P("seg", "sub", None, None, None, None),
        P("seg", "sub", None, None),
        P("seg", None, None),
        P("seg", None, None),
        P("seg", None, None),
    )
    out_specs = (P("seg", "sub", None, None, None), P("seg", None, None))
    return jax.shard_map(shards, mesh=mesh, in_specs=in_specs, out_specs=out_specs, check_vma=False)
```
